512 devices in a mesh: dp: 64 (over z_lo, y, core), tensor: 8 (over z_hi, x).
Axes of the slice: x: 4, y: 4, z: 16 (z_hi: 2, z_lo: 8; z = z_hi * 8 + z_lo), core: 2. Of those that a mesh axis runs over, the one named last changes fastest.
Arguments:
- tokens: bfloat16 [16384, 1024], P('dp'), may hold values from -6 to 6
- hidden_grad: bfloat16 [16384, 14336], P('dp', 'tensor'), may hold values from -6 to 6
- gate: bfloat16 [16384, 14336], P('dp', 'tensor'), may hold values from -8 to 8
- up: bfloat16 [16384, 14336], P('dp', 'tensor'), may hold values from -6 to 6
- gate_weight: bfloat16 [1024, 14336], P('dp', 'tensor'), may hold values from -0.046875 to 0.046875
- up_weight: bfloat16 [1024, 14336], P('dp', 'tensor'), may hold values from -0.046875 to 0.046875
Outputs:
- input_grad: bfloat16 [16384, 1024], P('dp', 'tensor')
- act_cov: float32 [1024, 1024], P('tensor')
- grad_cov: float32 [1024, 1024], P('tensor')
The draws below stay inside these ranges and needn't reach their ends.
All inputs are finite; a program needn't handle non-finite values.
Results may differ from the reference program's by a relative error of at most 0.0049.
Values may be sent and summed in bfloat16 or wider, within the bound.
A program may use at most 64 MiB of HBM per device.

```python
import jax
import jax.numpy as jnp
from jax import lax

BLOCK = 1024
FFW = 14336
TOK_DEV = 256
TOKENS = 16384
N_DP = 64


def level_of(key, shape, cuts, smallest, high):
    gain, own = 1.0, jax.random.fold_in(key, 6)
    for position, blocks in cuts:
        draws = jnp.exp(jax.random.uniform(jax.random.fold_in(own, position), (blocks,), jnp.float32, smallest / len(cuts), high / len(cuts)))
        gain = gain * jnp.repeat(draws, shape[position] // blocks).reshape([-1 if axis == position else 1 for axis in range(len(shape))])
    return gain


def centred(own_key, shape, deviation, limit, split=(), kind=jnp.bfloat16):
    entries = deviation * jax.random.normal(own_key, shape, jnp.float32)
    if split:
        entries = entries * level_of(own_key, shape, split, -0.22, 0.18)
    return jnp.clip(entries, -limit, limit).astype(kind)


def setup_inputs(seed: int = 0) -> dict:
    streams_of = jax.random.split(jax.random.key(seed), 7)
    return {
        "tokens": centred(streams_of[0], (TOKENS, BLOCK), 1.0, 6.0, ((0, 64),)),
        "hidden_grad": centred(streams_of[1], (TOKENS, FFW), 1.0, 6.0, ((0, 64), (1, 8))),
        "gate": centred(streams_of[2], (TOKENS, FFW), 1.5, 8.0, ((0, 64), (1, 8))),
        "up": centred(streams_of[3], (TOKENS, FFW), 1.0, 6.0, ((0, 64), (1, 8))),
        "gate_weight": centred(streams_of[4], (BLOCK, FFW), FFW ** -0.5, 0.046875, ((0, 64), (1, 8))),
        "up_weight": centred(streams_of[5], (BLOCK, FFW), FFW ** -0.5, 0.046875, ((0, 64), (1, 8))),
    }


def backward_rows(hidden_grad, gate, up, gate_weight, up_weight):
    grad32 = hidden_grad.astype(jnp.float32)
    gate32 = gate.astype(jnp.float32)
    up32 = up.astype(jnp.float32)
    sig = jax.nn.sigmoid(gate32)
    grad_gate = (grad32 * up32 * sig * (1.0 + gate32 * (1.0 - sig))).astype(jnp.bfloat16)
    grad_up = (grad32 * gate32 * sig).astype(jnp.bfloat16)
    dims = (((1,), (1,)), ((), ()))
    total = lax.dot_general(grad_gate, gate_weight, dims, preferred_element_type=jnp.float32)
    total = total + lax.dot_general(grad_up, up_weight, dims, preferred_element_type=jnp.float32)
    return total.astype(jnp.bfloat16)


def reference(tokens, hidden_grad, gate, up, gate_weight, up_weight):
    count = TOK_DEV * N_DP

    def one_block(items):
        return backward_rows(items[0], items[1], items[2], gate_weight, up_weight)

    blocks = lax.map(one_block, (hidden_grad.reshape(N_DP, TOK_DEV, FFW), gate.reshape(N_DP, TOK_DEV, FFW), up.reshape(N_DP, TOK_DEV, FFW)))
    input_grad = blocks.reshape(count, BLOCK)
    act_cov = jnp.dot(tokens.T, tokens, preferred_element_type=jnp.float32) / count
    grad_cov = jnp.dot(input_grad.T, input_grad, preferred_element_type=jnp.float32) / count
    return input_grad, act_cov, grad_cov
```

```python
import jax
import jax.numpy as jnp
from jax import lax
from jax.experimental import pallas as pl
from jax.experimental.pallas import tpu as pltpu
from jax.sharding import PartitionSpec as P

BF16 = jnp.bfloat16
F32 = jnp.float32
NT = (((1,), (1,)), ((), ()))
TN = (((0,), (0,)), ((), ()))
COUNT = 16384


def kernel(
    tok_hbm, hid_hbm, gate_hbm, up_hbm, gw_hbm, uw_hbm,
    ig_out, act_out, cov_out,
    tok, vin, acts, w, pown, xs, xr, zsb, zrb, gbuf, swp, gfull,
    covp, d0r, d1s, d1r, d2s, d2r, fin,
    loc_sem, as_s, as_r, zs_s, z_r, ys_s, y_r, y2s_s, y2_r,
    xs_s, xs_r, z8_s, z8_r, sw_s, sw_r, xg_s, xg_r,
    d0_s, d0_r, d1_s, d1_r, d2_s, d2_r, d3_s, d3_r, d4_s, d4_r, d5_s, d5_r,
):
    i = lax.axis_index("dp")
    j = lax.axis_index("tensor")
    c = lax.rem(i, 2)
    y = lax.rem(lax.div(i, 2), 4)
    z = lax.div(i, 8)
    x = lax.rem(j, 4)
    zh = lax.div(j, 4)
    oc = 1 - c

    def dev(z_=z, y_=y, c_=c, zh_=zh, x_=x):
        return ((z_ * 4 + y_) * 2 + c_, zh_ * 4 + x_)

    def remote(src, dst, ss, rs, to):
        return pltpu.make_async_remote_copy(
            src_ref=src, dst_ref=dst, send_sem=ss, recv_sem=rs,
            device_id=to, device_id_type=pl.DeviceIdType.MESH,
        )

    sib = dev(c_=oc)

    def ymod(k):
        return lax.rem(y + k, 4)

    def xmod(k):
        return lax.rem(x + k, 4)

    def zmod(k):
        return lax.rem(z + k, 8)

    def chunk(zz, yy):
        return w.at[lax.rem(zz, 4), :, lax.div(zz, 4), yy]

    def half(zz, yy, g):
        return w.at[lax.rem(zz, 4), g, lax.div(zz, 4), yy]

    loads = [
        pltpu.make_async_copy(gw_hbm, half(z, y, 0), loc_sem.at[0]),
        pltpu.make_async_copy(uw_hbm, half(z, y, 1), loc_sem.at[1]),
        pltpu.make_async_copy(hid_hbm, vin.at[0], loc_sem.at[2]),
        pltpu.make_async_copy(gate_hbm, vin.at[1], loc_sem.at[3]),
        pltpu.make_async_copy(up_hbm, vin.at[2], loc_sem.at[4]),
        pltpu.make_async_copy(tok_hbm, tok, loc_sem.at[5]),
    ]
    for load in loads:
        load.start()

    barrier = pltpu.get_barrier_semaphore()
    partners = [sib]
    partners += [dev(y_=ymod(k)) for k in range(1, 4)]
    partners += [dev(x_=xmod(k)) for k in range(1, 4)]
    partners += [dev(z_=zmod(k)) for k in range(1, 8)]
    partners += [dev(zh_=1 - zh)]
    for to in partners:
        pl.semaphore_signal(
            barrier, inc=1, device_id=to, device_id_type=pl.DeviceIdType.MESH
        )
    for load in loads:
        load.wait()

    def act_rows(r, _):
        rows = pl.ds(pl.multiple_of(r * 16, 16), 16)
        h32 = vin[0, rows, :].astype(F32)
        g32 = vin[1, rows, :].astype(F32)
        u32 = vin[2, rows, :].astype(F32)
        sig = jax.nn.sigmoid(g32)
        hs = h32 * sig
        acts[c, 0, rows, :] = (hs * u32 * (1.0 + g32 * (1.0 - sig))).astype(BF16)
        acts[c, 1, rows, :] = (hs * g32).astype(BF16)
        return 0

    lax.fori_loop(0, 16, act_rows, 0)

    own_tok = tok[:, pl.ds(pl.multiple_of(j * 128, 128), 128)]
    for k in range(8):
        covp[0, k] = lax.dot_general(
            own_tok, tok[:, k * 128:(k + 1) * 128], TN, preferred_element_type=F32
        )

    pl.semaphore_wait(barrier, 15)

    def z_up(zz):
        return remote(chunk(zz, y), chunk(zz, y), zs_s.at[0, zz], z_r.at[zz], dev(z_=z + 1))

    def z_dn(zz):
        return remote(chunk(zz, y), chunk(zz, y), zs_s.at[1, zz], z_r.at[zz], dev(z_=z - 1))

    def y_send(zz, d):
        to = dev(y_=ymod(1 if d == 0 else 3))
        return remote(chunk(zz, y), chunk(zz, y), ys_s.at[d, zz], y_r.at[d, zz], to)

    def y_recv(zz, d):
        src = ymod(3 if d == 0 else 1)
        return remote(chunk(zz, src), chunk(zz, src), ys_s.at[d, zz], y_r.at[d, zz], sib)

    def y2_send(zz, d):
        src = ymod(3 if d == 0 else 1)
        to = dev(y_=ymod(1 if d == 0 else 3))
        return remote(half(zz, src, d), half(zz, src, d), y2s_s.at[d, zz], y2_r.at[d, zz], to)

    def y2_recv(zz, d):
        src = ymod(2)
        return remote(half(zz, src, d), half(zz, src, d), y2s_s.at[d, zz], y2_r.at[d, zz], sib)

    def each(s, fn):
        @pl.when((s >= 0) & (z - s >= 0) & (z - s <= 7))
        def _():
            fn(z - s, 0)

        @pl.when((s >= 1) & (z + s <= 7))
        def _():
            fn(z + s, 1)

    def arrive_z(s):
        def fn(zz, d):
            @pl.when(s > 0)
            def _():
                remote(chunk(zz, y), chunk(zz, y), zs_s.at[0, zz], z_r.at[zz], sib).wait_recv()

            if d == 0:
                @pl.when(z < 7)
                def _():
                    z_up(zz).start()

                @pl.when((s == 0) & (z > 0))
                def _():
                    z_dn(zz).start()
            else:
                @pl.when(z > 0)
                def _():
                    z_dn(zz).start()
            y_send(zz, 0).start()
            y_send(zz, 1).start()
        return fn

    def arrive_y(zz, _):
        for d in range(2):
            y_recv(zz, d).wait_recv()
            y2_send(zz, d).start()

    def arrive_y2(zz, _):
        for d in range(2):
            y2_recv(zz, d).wait_recv()

    def ready(t):
        below = jnp.abs(z - t)
        above = jnp.abs(z - t - 4)
        return jnp.maximum(below, above)

    def x_send(t):
        return remote(xs.at[t], xr.at[x], xs_s.at[t], xs_r.at[x], dev(x_=t))

    def block(t, s):
        @pl.when(ready(t) == s)
        def _():
            wg = w[t, 0].reshape(128, 1792)
            wu = w[t, 1].reshape(128, 1792)
            for cc in range(2):
                part = lax.dot_general(acts[cc, 0], wg, NT, preferred_element_type=F32)
                part += lax.dot_general(acts[cc, 1], wu, NT, preferred_element_type=F32)

                @pl.when(t == x)
                def _():
                    pown[cc] = part

                @pl.when(t != x)
                def _():
                    xs[t, cc] = part.astype(BF16)

            @pl.when(t != x)
            def _():
                x_send(t).start()
        return s

    z8 = remote(zsb, zrb, z8_s, z8_r, dev(zh_=1 - zh))
    act_copy = remote(acts.at[c], acts.at[c], as_s, as_r, sib)
    act_back = remote(acts.at[oc], acts.at[oc], as_s, as_r, sib)

    def x_sum():
        for k in range(1, 4):
            src = xmod(k)
            remote(xs.at[0], xr.at[src], xs_s.at[src], xs_r.at[src], sib).wait_recv()
        for cc in range(2):
            total = pown[cc]
            for k in range(1, 4):
                total = total + xr[xmod(k), cc].astype(F32)
            pown[cc] = total
            zsb[cc] = total.astype(BF16)
        z8.start()

    def step(s, _):
        each(s, arrive_z(s))

        @pl.when(s == 0)
        def _():
            act_copy.start()
            d0_send(0).start()

        each(s - 1, arrive_y)

        @pl.when(s == 2)
        def _():
            act_back.wait_recv()

        each(s - 2, arrive_y2)
        lax.fori_loop(0, 4, block, s - 2)

        @pl.when(ready(x) == s - 3)
        def _():
            x_sum()
        return 0

    def d0_send(m):
        rows = pl.ds(pl.multiple_of(oc * 64, 64), 64)
        return remote(covp.at[m, :, rows], d0r.at[m], d0_s.at[m], d0_r.at[m], sib)

    def d1_send(m, k):
        to = ymod(k)
        return remote(d1s.at[m, to], d1r.at[m, y], d1_s.at[m, to], d1_r.at[m, y], dev(y_=to))

    def d1_recv(m, k):
        src = ymod(k)
        return remote(d1s.at[m, src], d1r.at[m, src], d1_s.at[m, src], d1_r.at[m, src], sib)

    def d2_send(m, k):
        to = zmod(k)
        return remote(d2s.at[m, to], d2r.at[m, z], d2_s.at[m, to], d2_r.at[m, z], dev(z_=to))

    def d2_recv(m, k):
        src = zmod(k)
        return remote(d2s.at[m, src], d2r.at[m, src], d2_s.at[m, src], d2_r.at[m, src], sib)

    def d3_send(m, k):
        to = zmod(k)
        piece = fin.at[m, c, y, z]
        return remote(piece, piece, d3_s.at[m, to], d3_r.at[m, z], dev(z_=to))

    def d3_recv(m, k):
        src = zmod(k)
        piece = fin.at[m, c, y, src]
        return remote(piece, piece, d3_s.at[m, src], d3_r.at[m, src], sib)

    def d4_send(m, k):
        to = ymod(k)
        piece = fin.at[m, c, y]
        return remote(piece, piece, d4_s.at[m, to], d4_r.at[m, y], dev(y_=to))

    def d4_recv(m, k):
        src = ymod(k)
        piece = fin.at[m, c, src]
        return remote(piece, piece, d4_s.at[m, src], d4_r.at[m, src], sib)

    def d5_send(m):
        return remote(fin.at[m, c], fin.at[m, c], d5_s.at[m], d5_r.at[m], sib)

    def d5_recv(m):
        return remote(fin.at[m, oc], fin.at[m, oc], d5_s.at[m], d5_r.at[m], sib)

    def core_sum(m):
        d0_send(m).wait_recv()
        for yy in range(4):
            rows = pl.ds(pl.multiple_of(c * 64 + yy * 16, 16), 16)
            total = covp[m, :, rows, :] + d0r[m, :, yy * 16:(yy + 1) * 16, :]
            covp[m, :, rows, :] = total
            d1s[m, yy] = total.astype(BF16)
        for k in (2, 1, 3):
            d1_send(m, k).start()

    def y_sum(m):
        rows = pl.ds(pl.multiple_of(c * 64 + y * 16, 16), 16)
        total = covp[m, :, rows, :]
        for k in (1, 3, 2):
            d1_recv(m, k).wait_recv()
            total = total + d1r[m, ymod(k)].astype(F32)
        covp[m, :, rows, :] = total
        d2s[m] = total.astype(BF16)
        for k in range(1, 8):
            d2_send(m, k).start()

    def z_sum(m):
        rows = pl.ds(pl.multiple_of(c * 64 + y * 16, 16), 16)
        total = covp[m, z, rows, :]
        for k in range(1, 8):
            d2_recv(m, k).wait_recv()
            total = total + d2r[m, zmod(k)].astype(F32)
        fin[m, c, y, z] = (total * (1.0 / COUNT)).astype(BF16)
        for k in range(1, 8):
            d3_send(m, k).start()

    def z_back(m):
        for k in range(1, 8):
            d3_recv(m, k).wait_recv()
        for k in (2, 1, 3):
            d4_send(m, k).start()

    def y_back(m):
        for k in (1, 3, 2):
            d4_recv(m, k).wait_recv()
        d5_send(m).start()

    def write(m, out, cc):
        for yy in range(4):
            rows = pl.ds(pl.multiple_of(cc * 64 + yy * 16, 16), 16)
            for k in range(8):
                out[rows, k * 128:(k + 1) * 128] = fin[m, cc, yy, k].astype(F32)

    lax.fori_loop(0, 11, step, 0)

    core_sum(0)
    y_sum(0)

    z8.wait_recv()
    for cc in range(2):
        gbuf[cc] = (pown[cc] + zrb[cc].astype(F32)).astype(BF16)
    swap = remote(gbuf.at[oc], swp, sw_s, sw_r, sib)
    swap.start()

    src_i = lax.broadcasted_iota(jnp.int32, (256, 256), 0)
    dst_i = lax.broadcasted_iota(jnp.int32, (256, 256), 1)
    d_half, d_y = lax.div(dst_i, 128), lax.rem(lax.div(dst_i, 32), 4)
    d_core, d_row = lax.rem(lax.div(dst_i, 16), 2), lax.rem(dst_i, 16)
    own_first = lax.rem(d_core + c, 2)
    perm = (src_i == own_first * 128 + d_half * 64 + d_y * 16 + d_row).astype(F32).astype(BF16)

    swap.wait_recv()
    own_half = gbuf[c]
    both = lax.dot_general(
        own_half, perm[:128], (((1,), (0,)), ((), ())), preferred_element_type=F32
    ) + lax.dot_general(
        swp[...], perm[128:], (((1,), (0,)), ((), ())), preferred_element_type=F32
    )
    gfull[x] = both.astype(BF16)

    def xg_send(k):
        to = xmod(k)
        return remote(gfull.at[x], gfull.at[x], xg_s.at[to], xg_r.at[x], dev(x_=to))

    def xg_recv(k):
        src = xmod(k)
        return remote(gfull.at[src], gfull.at[src], xg_s.at[src], xg_r.at[src], sib)

    for k in (2, 1, 3):
        xg_send(k).start()
    own = gfull[x, :, pl.ds(pl.multiple_of(zh * 128, 128), 128)]
    ig_out[...] = own

    def cov_cols(k):
        xx = xmod(k)
        part = lax.dot_general(own, gfull[xx], TN, preferred_element_type=F32)
        covp[1, xx] = part[:, :128]
        covp[1, xx + 4] = part[:, 128:]

    cov_cols(0)
    z_sum(0)
    for k in (1, 3, 2):
        xg_recv(k).wait_recv()
        cov_cols(k)
    d0_send(1).start()
    core_sum(1)
    z_back(0)
    y_sum(1)
    y_back(0)
    write(0, act_out, c)
    d5_recv(0).wait_recv()
    write(0, act_out, oc)
    z_sum(1)
    z_back(1)
    y_back(1)
    write(1, cov_out, c)
    d5_recv(1).wait_recv()
    write(1, cov_out, oc)

    act_copy.wait_send()
    z8.wait_send()
    swap.wait_send()

    def drain(zz, _):
        @pl.when((z < 7) & (zz <= z))
        def _():
            z_up(zz).wait_send()

        @pl.when((z > 0) & (zz >= z))
        def _():
            z_dn(zz).wait_send()

        for d in range(2):
            y_send(zz, d).wait_send()
            y2_send(zz, d).wait_send()
        return 0

    lax.fori_loop(0, 8, drain, 0)
    for k in range(1, 4):
        x_send(xmod(k)).wait_send()
        xg_send(k).wait_send()
    for m in range(2):
        d0_send(m).wait_send()
        for k in range(1, 4):
            d1_send(m, k).wait_send()
            d4_send(m, k).wait_send()
        for k in range(1, 8):
            d2_send(m, k).wait_send()
            d3_send(m, k).wait_send()
        d5_send(m).wait_send()


def shards(tokens, hidden_grad, gate, up, gate_weight, up_weight):
    sem = pltpu.SemaphoreType.DMA
    return pl.pallas_call(
        kernel,
        out_shape=(
            jax.ShapeDtypeStruct((256, 128), BF16),
            jax.ShapeDtypeStruct((128, 1024), F32),
            jax.ShapeDtypeStruct((128, 1024), F32),
        ),
        in_specs=[pl.BlockSpec(memory_space=pl.ANY)] * 6,
        out_specs=tuple([pl.BlockSpec(memory_space=pltpu.VMEM)] * 3),
        scratch_shapes=[
            pltpu.VMEM((256, 1024), BF16),
            pltpu.VMEM((3, 256, 1792), BF16),
            pltpu.VMEM((2, 2, 256, 1792), BF16),
            pltpu.VMEM((4, 2, 2, 4, 16, 1792), BF16),
            pltpu.VMEM((2, 256, 128), F32),
            pltpu.VMEM((4, 2, 256, 128), BF16),
            pltpu.VMEM((4, 2, 256, 128), BF16),
            pltpu.VMEM((2, 256, 128), BF16),
            pltpu.VMEM((2, 256, 128), BF16),
            pltpu.VMEM((2, 256, 128), BF16),
            pltpu.VMEM((256, 128), BF16),
            pltpu.VMEM((4, 256, 256), BF16),
            pltpu.VMEM((2, 8, 128, 128), F32),
            pltpu.VMEM((2, 8, 64, 128), F32),
            pltpu.VMEM((2, 4, 8, 16, 128), BF16),
            pltpu.VMEM((2, 4, 8, 16, 128), BF16),
            pltpu.VMEM((2, 8, 16, 128), BF16),
            pltpu.VMEM((2, 8, 16, 128), BF16),
            pltpu.VMEM((2, 2, 4, 8, 16, 128), BF16),
            sem((6,)), sem, sem,
            sem((2, 8)), sem((8,)),
            sem((2, 8)), sem((2, 8)),
            sem((2, 8)), sem((2, 8)),
            sem((4,)), sem((4,)),
            sem, sem, sem, sem,
            sem((4,)), sem((4,)),
            sem((2,)), sem((2,)),
            sem((2, 4)), sem((2, 4)),
            sem((2, 8)), sem((2, 8)),
            sem((2, 8)), sem((2, 8)),
            sem((2, 4)), sem((2, 4)),
            sem((2,)), sem((2,)),
        ],
        compiler_params=pltpu.CompilerParams(
            collective_id=1, has_side_effects=True, vmem_limit_bytes=44 << 20
        ),
        cost_estimate=pl.CostEstimate(
            flops=2_500_000_000, bytes_accessed=10_000_000, transcendentals=1_000_000
        ),
        name="kfac_stats",
    )(tokens, hidden_grad, gate, up, gate_weight, up_weight)


def solution(mesh):
    placed = (
        P("dp", None),
        P("dp", "tensor"),
        P("dp", "tensor"),
        P("dp", "tensor"),
        P("dp", "tensor"),
        P("dp", "tensor"),
    )
    return jax.shard_map(
        shards,
        mesh=mesh,
        in_specs=placed,
        out_specs=(P("dp", "tensor"), P("tensor", None), P("tensor", None)),
        check_vma=False,
    )
```

```python
import jax
import jax.numpy as jnp
from jax import lax
from jax.experimental import pallas as pl
from jax.experimental.pallas import tpu as pltpu
from jax.sharding import PartitionSpec as P

BF16 = jnp.bfloat16
F32 = jnp.float32
NT = (((1,), (1,)), ((), ()))
TN = (((0,), (0,)), ((), ()))
COUNT = 16384
LAG = 3
STOP = 9


def kernel(
    tok_hbm, hid_hbm, gate_hbm, up_hbm, gw_hbm, uw_hbm,
    fin_out, own_out,
    tok, vin, acts, w, pown, xs, xr, zsb, zrb, gs, gt,
    covp, d0r, d1s, d1r, d2s, d2r, fin,
    loc_sem, as_s, as_r, zs_s, z_r, ys_s, y_r, y2s_s, y2_r,
    xs_s, xs_r, z8_s, z8_r, xg_s, xg_r, out_sem,
    d0_s, d0_r, d1_s, d1_r, d2_s, d2_r, d3_s, d3_r, d4_s, d4_r, d5_s, d5_r, hello_sem,
):
    i = lax.axis_index("dp")
    j = lax.axis_index("tensor")
    c = lax.rem(i, 2)
    y = lax.rem(lax.div(i, 2), 4)
    z = lax.div(i, 8)
    x = lax.rem(j, 4)
    zh = lax.div(j, 4)
    oc = 1 - c

    def dev(z_=z, y_=y, c_=c, zh_=zh, x_=x):
        return ((z_ * 4 + y_) * 2 + c_, zh_ * 4 + x_)

    def remote(src, dst, ss, rs, to):
        return pltpu.make_async_remote_copy(
            src_ref=src, dst_ref=dst, send_sem=ss, recv_sem=rs,
            device_id=to, device_id_type=pl.DeviceIdType.MESH,
        )

    sib = dev(c_=oc)

    def ymod(k):
        return lax.rem(y + k, 4)

    def xmod(k):
        return lax.rem(x + k, 4)

    def zmod(k):
        return lax.rem(z + k, 8)

    def chunk(zz, yy):
        return w.at[lax.rem(zz, 4), :, lax.div(zz, 4), yy]

    def half(zz, yy, g):
        return w.at[lax.rem(zz, 4), g, lax.div(zz, 4), yy]

    loads = [
        pltpu.make_async_copy(gw_hbm, half(z, y, 0), loc_sem.at[0]),
        pltpu.make_async_copy(uw_hbm, half(z, y, 1), loc_sem.at[1]),
        pltpu.make_async_copy(hid_hbm, vin.at[0], loc_sem.at[2]),
        pltpu.make_async_copy(gate_hbm, vin.at[1], loc_sem.at[3]),
        pltpu.make_async_copy(up_hbm, vin.at[2], loc_sem.at[4]),
        pltpu.make_async_copy(tok_hbm, tok, loc_sem.at[5]),
    ]
    for load in loads:
        load.start()

    barrier = pltpu.get_barrier_semaphore()
    zf = zh * 8 + z

    def ring(k):
        to = lax.rem(zf + k, 16)
        return dev(z_=lax.rem(to, 8), zh_=lax.div(to, 8))

    partners = [sib] + [ring(k) for k in (1, 15, 2, 14)]
    partners += [dev(y_=ymod(k)) for k in range(1, 4)]
    partners += [dev(x_=xmod(k)) for k in range(1, 4)]
    for to in partners:
        pl.semaphore_signal(
            barrier, inc=1, device_id=to, device_id_type=pl.DeviceIdType.MESH
        )
    for load in loads[:2]:
        load.wait()

    def act_rows(r, _):
        rows = pl.ds(pl.multiple_of(r * 16, 16), 16)
        h32 = vin[0, rows, :].astype(F32)
        g32 = vin[1, rows, :].astype(F32)
        u32 = vin[2, rows, :].astype(F32)
        sig = jax.nn.sigmoid(g32)
        hs = h32 * sig
        acts[c, 0, rows, :] = (hs * u32 * (1.0 + g32 * (1.0 - sig))).astype(BF16)
        acts[c, 1, rows, :] = (hs * g32).astype(BF16)
        return 0

    def token_cov(k):
        own_tok = tok[:, pl.ds(pl.multiple_of(j * 128, 128), 128)]
        cols = tok[:, pl.ds(pl.multiple_of(k * 128, 128), 128)]
        covp[0, k] = lax.dot_general(own_tok, cols, TN, preferred_element_type=F32)

    def act_send(r):
        rows = pl.ds(pl.multiple_of(r * 64, 64), 64)
        piece = acts.at[c, :, rows]
        return remote(piece, piece, as_s.at[r], as_r.at[r], sib)

    def act_recv(r):
        rows = pl.ds(pl.multiple_of(r * 64, 64), 64)
        piece = acts.at[oc, :, rows]
        return remote(piece, piece, as_s.at[r], as_r.at[r], sib)

    def local_part(s):
        @pl.when(s < 4)
        def _():
            @pl.when(s == 0)
            def _():
                for load in loads[2:5]:
                    load.wait()

            def rows4(r, _):
                act_rows(s * 4 + r, 0)
                return 0

            lax.fori_loop(0, 4, rows4, 0)
            act_send(s).start()

        @pl.when((s >= 4) & (s < 8))
        def _():
            @pl.when(s == 4)
            def _():
                loads[5].wait()

            token_cov(s * 2 - 8)
            token_cov(s * 2 - 7)

            @pl.when(s == 7)
            def _():
                d0_send(0).start()

    pl.semaphore_wait(barrier, 11)

    def z_up(zz, g):
        return remote(
            half(zz, y, g), half(zz, y, g), zs_s.at[0, g, zz], z_r.at[g, zz], dev(z_=z + 1)
        )

    def z_dn(zz, g):
        return remote(
            half(zz, y, g), half(zz, y, g), zs_s.at[1, g, zz], z_r.at[g, zz], dev(z_=z - 1)
        )

    def y_send(zz, d, g):
        to = dev(y_=ymod(1 if d == 0 else 3))
        return remote(
            half(zz, y, g), half(zz, y, g), ys_s.at[d, g, zz], y_r.at[d, g, zz], to
        )

    def y_recv(zz, d, g):
        src = ymod(3 if d == 0 else 1)
        return remote(
            half(zz, src, g), half(zz, src, g), ys_s.at[d, g, zz], y_r.at[d, g, zz], sib
        )

    def y2_send(zz, d):
        src = ymod(3 if d == 0 else 1)
        to = dev(y_=ymod(1 if d == 0 else 3))
        return remote(half(zz, src, d), half(zz, src, d), y2s_s.at[d, zz], y2_r.at[d, zz], to)

    def y2_recv(zz, d):
        src = ymod(2)
        return remote(half(zz, src, d), half(zz, src, d), y2s_s.at[d, zz], y2_r.at[d, zz], sib)

    def each(s, fn):
        @pl.when((s >= 0) & (z - s >= 0) & (z - s <= 7))
        def _():
            fn(z - s, 0)

        @pl.when((s >= 1) & (z + s <= 7))
        def _():
            fn(z + s, 1)

    def arrive_z(s):
        def fn(zz, d):
            for g in range(2):
                @pl.when(s > 0)
                def _():
                    remote(
                        half(zz, y, g), half(zz, y, g), zs_s.at[0, g, zz], z_r.at[g, zz], sib
                    ).wait_recv()

                if d == 0:
                    @pl.when(z < 7)
                    def _():
                        z_up(zz, g).start()

                    @pl.when((s == 0) & (z > 0))
                    def _():
                        z_dn(zz, g).start()
                else:
                    @pl.when(z > 0)
                    def _():
                        z_dn(zz, g).start()
                y_send(zz, g, g).start()
                y_send(zz, 1 - g, g).start()
        return fn

    def arrive_y(zz, _):
        for d in range(2):
            y_recv(zz, d, d).wait_recv()
            y2_send(zz, d).start()

    def arrive_y2(zz, _):
        for d in range(2):
            y_recv(zz, d, 1 - d).wait_recv()
            y2_recv(zz, d).wait_recv()
        project(zz)

    def x_send(zz):
        to, hh = lax.rem(zz, 4), lax.div(zz, 4)
        return remote(xs.at[zz], xr.at[hh, x], xs_s.at[zz], xs_r.at[hh, x], dev(x_=to))

    def x_recv(k, hh):
        src = xmod(k)
        return remote(xs.at[src], xr.at[hh, src], xs_s.at[src], xs_r.at[hh, src], sib)

    def project(zz):
        t, hh = lax.rem(zz, 4), lax.div(zz, 4)
        wg = w[t, 0, hh].reshape(64, 1792)
        wu = w[t, 1, hh].reshape(64, 1792)
        for cc in range(2):
            part = lax.dot_general(wg, acts[cc, 0], NT, preferred_element_type=F32)
            part += lax.dot_general(wu, acts[cc, 1], NT, preferred_element_type=F32)

            @pl.when(t == x)
            def _():
                pown[hh, cc] = part

            @pl.when(t != x)
            def _():
                xs[zz, cc] = part.astype(BF16)

        @pl.when(t != x)
        def _():
            x_send(zz).start()

    def z8(hh):
        return remote(zsb.at[hh], zrb.at[hh], z8_s.at[hh], z8_r.at[hh], dev(zh_=1 - zh))


    def x_sum(hh):
        for k in range(1, 4):
            x_recv(k, hh).wait_recv()
        for cc in range(2):
            total = pown[hh, cc]
            for k in range(1, 4):
                total = total + xr[hh, xmod(k), cc].astype(F32)
            pown[hh, cc] = total
            zsb[hh, cc] = total.astype(BF16)
        z8(hh).start()

    def hello():
        pl.semaphore_signal(
            hello_sem, inc=1, device_id=ring(2), device_id_type=pl.DeviceIdType.MESH
        )

    def step(s, _):
        @pl.when(s < 4)
        def _():
            hello()

        each(s, arrive_z(s))

        local_part(s)

        each(s - 1, arrive_y)

        @pl.when(s == LAG)
        def _():
            for r in range(4):
                act_recv(r).wait_recv()

        each(s - LAG, arrive_y2)

        def own_sum(hh, _):
            @pl.when(jnp.abs(z - x - 4 * hh) == s - LAG - 1)
            def _():
                x_sum(hh)
            return 0

        lax.fori_loop(0, 2, own_sum, 0)

        @pl.when(s < 4)
        def _():
            pl.semaphore_wait(hello_sem, 1)
        return 0

    def d0_send(m):
        rows = pl.ds(pl.multiple_of(oc * 64, 64), 64)
        return remote(covp.at[m, :, rows], d0r.at[m], d0_s.at[m], d0_r.at[m], sib)

    def d1_send(m, k):
        to = ymod(k)
        return remote(d1s.at[m, to], d1r.at[m, y], d1_s.at[m, to], d1_r.at[m, y], dev(y_=to))

    def d1_recv(m, k):
        src = ymod(k)
        return remote(d1s.at[m, src], d1r.at[m, src], d1_s.at[m, src], d1_r.at[m, src], sib)

    def d2_send(m, k):
        to = zmod(k)
        return remote(d2s.at[m, to], d2r.at[m, z], d2_s.at[m, to], d2_r.at[m, z], dev(z_=to))

    def d2_recv(m, k):
        src = zmod(k)
        return remote(d2s.at[m, src], d2r.at[m, src], d2_s.at[m, src], d2_r.at[m, src], sib)

    def d3_send(m, k):
        to = zmod(k)
        piece = fin.at[m, c, y, z]
        return remote(piece, piece, d3_s.at[m, to], d3_r.at[m, z], dev(z_=to))

    def d3_recv(m, k):
        src = zmod(k)
        piece = fin.at[m, c, y, src]
        return remote(piece, piece, d3_s.at[m, src], d3_r.at[m, src], sib)

    def d4_send(m, k):
        to = ymod(k)
        piece = fin.at[m, c, y]
        return remote(piece, piece, d4_s.at[m, to], d4_r.at[m, y], dev(y_=to))

    def d4_recv(m, k):
        src = ymod(k)
        piece = fin.at[m, c, src]
        return remote(piece, piece, d4_s.at[m, src], d4_r.at[m, src], sib)

    def d5_send(m):
        return remote(fin.at[m, c], fin.at[m, c], d5_s.at[m], d5_r.at[m], sib)

    def d5_recv(m):
        return remote(fin.at[m, oc], fin.at[m, oc], d5_s.at[m], d5_r.at[m], sib)

    def core_sum(m):
        d0_send(m).wait_recv()
        for yy in range(4):
            rows = pl.ds(pl.multiple_of(c * 64 + yy * 16, 16), 16)
            total = covp[m, :, rows, :] + d0r[m, :, yy * 16:(yy + 1) * 16, :]
            covp[m, :, rows, :] = total
            d1s[m, yy] = total.astype(BF16)
        for k in (2, 1, 3):
            d1_send(m, k).start()

    def y_sum(m):
        rows = pl.ds(pl.multiple_of(c * 64 + y * 16, 16), 16)
        total = covp[m, :, rows, :]
        for k in (1, 3, 2):
            d1_recv(m, k).wait_recv()
            total = total + d1r[m, ymod(k)].astype(F32)
        covp[m, :, rows, :] = total
        d2s[m] = total.astype(BF16)
        for k in range(1, 8):
            d2_send(m, k).start()

    def z_sum(m):
        rows = pl.ds(pl.multiple_of(c * 64 + y * 16, 16), 16)
        total = covp[m, z, rows, :]
        for k in range(1, 8):
            d2_recv(m, k).wait_recv()
            total = total + d2r[m, zmod(k)].astype(F32)
        fin[m, c, y, z] = (total * (1.0 / COUNT)).astype(BF16)
        for k in range(1, 8):
            d3_send(m, k).start()

    def z_back(m):
        for k in range(1, 8):
            d3_recv(m, k).wait_recv()
        for k in (2, 1, 3):
            d4_send(m, k).start()

    def y_back(m):
        for k in (1, 3, 2):
            d4_recv(m, k).wait_recv()
        d5_send(m).start()

    def put(m, cc):
        return pltpu.make_async_copy(fin.at[m, cc], fin_out.at[m, cc], out_sem.at[m, cc])

    lax.fori_loop(0, 9 + LAG, step, 0)

    core_sum(0)
    y_sum(0)

    def drain(zz, _):
        for g in range(2):
            @pl.when((z < 7) & (zz <= z))
            def _():
                z_up(zz, g).wait_send()

            @pl.when((z > 0) & (zz >= z))
            def _():
                z_dn(zz, g).wait_send()

            for d in range(2):
                y_send(zz, d, g).wait_send()
            y2_send(zz, g).wait_send()
        return 0

    lax.fori_loop(0, 8, drain, 0)
    for r in range(4):
        act_send(r).wait_send()
    for k in range(1, 4):
        for hh in range(2):
            x_send(xmod(k) + 4 * hh).wait_send()

    def xg_send(k, cc, hh):
        to = xmod(k)
        return remote(
            gs.at[cc, hh], gt.at[hh, x, :, c], xg_s.at[to, cc, hh], xg_r.at[x, c, hh],
            dev(c_=cc, x_=to),
        )

    def xg_recv(k, cc, hh):
        src = xmod(k)
        return remote(
            gs.at[cc, hh], gt.at[hh, src, :, cc], xg_s.at[src, cc, hh], xg_r.at[src, cc, hh], sib
        )

    first = jnp.where(jnp.abs(z - x) <= jnp.abs(z - x - 4), 0, 1)
    for hh in (first, 1 - first):
        z8(hh).wait_recv()
        for cc in range(2):
            grad = (pown[hh, cc] + zrb[hh, cc].astype(F32)).astype(BF16)
            gs[cc, hh] = grad.reshape(4, 16, 256)
        xg_send(0, oc, hh).start()
        for k in (2, 1, 3):
            for cc in range(2):
                xg_send(k, cc, hh).start()
        mine = gs[c, hh]
        for yy in range(4):
            gt[hh, x, yy, c] = mine[yy]
    for hh in range(2):
        xg_recv(0, oc, hh).wait_recv()
    own = gt[zh, x].reshape(128, 256)
    own_out[...] = own

    def cov_cols(k):
        xx = xmod(k)
        for hh in range(2):
            covp[1, hh * 4 + xx] = lax.dot_general(
                own, gt[hh, xx].reshape(128, 256), NT, preferred_element_type=F32
            )

    cov_cols(0)
    z_sum(0)
    for k in (1, 3, 2):
        for cc in range(2):
            for hh in range(2):
                xg_recv(k, cc, hh).wait_recv()
        cov_cols(k)
    d0_send(1).start()
    z_back(0)
    core_sum(1)
    y_back(0)
    y_sum(1)
    put(0, c).start()
    d5_recv(0).wait_recv()
    put(0, oc).start()
    for hh in range(2):
        z8(hh).wait_send()
        xg_send(0, oc, hh).wait_send()
        for k in range(1, 4):
            for cc in range(2):
                xg_send(k, cc, hh).wait_send()

    def drain_sums(m):
        d0_send(m).wait_send()
        for k in range(1, 4):
            d1_send(m, k).wait_send()
        for k in range(1, 8):
            d2_send(m, k).wait_send()

    drain_sums(0)
    z_sum(1)
    for k in range(1, 4):
        d4_send(0, k).wait_send()
    for k in range(1, 8):
        d3_send(0, k).wait_send()
    d5_send(0).wait_send()
    for cc in (c, oc):
        put(0, cc).wait()
    z_back(1)
    drain_sums(1)
    y_back(1)
    put(1, c).start()
    for k in range(1, 8):
        d3_send(1, k).wait_send()
    for k in range(1, 4):
        d4_send(1, k).wait_send()
    d5_recv(1).wait_recv()
    put(1, oc).start()
    d5_send(1).wait_send()
    for cc in (c, oc):
        put(1, cc).wait()


def arrange(fin, own, ig_out, act_out, cov_out):
    ig_out[...] = own[...].astype(F32).T.astype(BF16)
    for m, out in enumerate((act_out, cov_out)):
        for q in range(8):
            for k in range(8):
                out[q * 16:(q + 1) * 16, k * 128:(k + 1) * 128] = fin[m, q // 4, q % 4, k].astype(F32)


def shards(tokens, hidden_grad, gate, up, gate_weight, up_weight):
    sem = pltpu.SemaphoreType.DMA
    fin, own = pl.pallas_call(
        kernel,
        out_shape=(
            jax.ShapeDtypeStruct((2, 2, 4, 8, 16, 128), BF16),
            jax.ShapeDtypeStruct((128, 256), BF16),
        ),
        in_specs=[pl.BlockSpec(memory_space=pltpu.HBM)] * 6,
        out_specs=(
            pl.BlockSpec(memory_space=pl.ANY),
            pl.BlockSpec(memory_space=pltpu.VMEM),
        ),
        scratch_shapes=[
            pltpu.VMEM((256, 1024), BF16),
            pltpu.VMEM((3, 256, 1792), BF16),
            pltpu.VMEM((2, 2, 256, 1792), BF16),
            pltpu.VMEM((4, 2, 2, 4, 16, 1792), BF16),
            pltpu.VMEM((2, 2, 64, 256), F32),
            pltpu.VMEM((8, 2, 64, 256), BF16),
            pltpu.VMEM((2, 4, 2, 64, 256), BF16),
            pltpu.VMEM((2, 2, 64, 256), BF16),
            pltpu.VMEM((2, 2, 64, 256), BF16),
            pltpu.VMEM((2, 2, 4, 16, 256), BF16),
            pltpu.VMEM((2, 4, 4, 2, 16, 256), BF16),
            pltpu.VMEM((2, 8, 128, 128), F32),
            pltpu.VMEM((2, 8, 64, 128), F32),
            pltpu.VMEM((2, 4, 8, 16, 128), BF16),
            pltpu.VMEM((2, 4, 8, 16, 128), BF16),
            pltpu.VMEM((2, 8, 16, 128), BF16),
            pltpu.VMEM((2, 8, 16, 128), BF16),
            pltpu.VMEM((2, 2, 4, 8, 16, 128), BF16),
            sem((6,)), sem((4,)), sem((4,)),
            sem((2, 2, 8)), sem((2, 8)),
            sem((2, 2, 8)), sem((2, 2, 8)),
            sem((2, 8)), sem((2, 8)),
            sem((8,)), sem((2, 4)),
            sem((2,)), sem((2,)),
            sem((4, 2, 2)), sem((4, 2, 2)), sem((2, 2)),
            sem((2,)), sem((2,)),
            sem((2, 4)), sem((2, 4)),
            sem((2, 8)), sem((2, 8)),
            sem((2, 8)), sem((2, 8)),
            sem((2, 4)), sem((2, 4)),
            sem((2,)), sem((2,)),
            pltpu.SemaphoreType.REGULAR,
        ],
        compiler_params=pltpu.CompilerParams(
            collective_id=1, has_side_effects=True, vmem_limit_bytes=60 << 20
        ),
        cost_estimate=pl.CostEstimate(
            flops=2_500_000_000, bytes_accessed=10_000_000, transcendentals=1_000_000
        ),
        name="kfac_stats",
    )(tokens, hidden_grad, gate, up, gate_weight, up_weight)
    return tuple(
        pl.pallas_call(
            arrange,
            out_shape=(
                jax.ShapeDtypeStruct((256, 128), BF16),
                jax.ShapeDtypeStruct((128, 1024), F32),
                jax.ShapeDtypeStruct((128, 1024), F32),
            ),
            in_specs=[pl.BlockSpec(memory_space=pltpu.VMEM)] * 2,
            out_specs=tuple([pl.BlockSpec(memory_space=pltpu.VMEM)] * 3),
            compiler_params=pltpu.CompilerParams(vmem_limit_bytes=16 << 20),
            name="arrange",
        )(fin, own)
    )


def solution(mesh):
    placed = (
        P("dp", None),
        P("dp", "tensor"),
        P("dp", "tensor"),
        P("dp", "tensor"),
        P("dp", "tensor"),
        P("dp", "tensor"),
    )
    return jax.shard_map(
        shards,
        mesh=mesh,
        in_specs=placed,
        out_specs=(P("dp", "tensor"), P("tensor", None), P("tensor", None)),
        check_vma=False,
    )
```

```python
import jax
import jax.numpy as jnp
from jax import lax
from jax.experimental import pallas as pl
from jax.experimental.pallas import tpu as pltpu
from jax.sharding import PartitionSpec as P

BF16 = jnp.bfloat16
F32 = jnp.float32
NT = (((1,), (1,)), ((), ()))
TN = (((0,), (0,)), ((), ()))
COUNT = 16384
LAG, CHAIN, HELLOS = 3, 6, 3
STOP = 9


def kernel(
    tok_hbm, hid_hbm, gate_hbm, up_hbm, gw_hbm, uw_hbm,
    fin_out, own_out,
    tok, vin, acts, w, pown, xs, xr, zsb, zrb, gs, gt,
    covp, d0r, d1s, d1r, d2s, d2r, fin,
    loc_sem, as_s, as_r, zs_s, z_r, ys_s, y_r, y2s_s, y2_r,
    xs_s, xs_r, z8_s, z8_r, xg_s, xg_r, out_sem,
    d0_s, d0_r, d1_s, d1_r, d2_s, d2_r, d3_s, d3_r, d4_s, d4_r, d5_s, d5_r, hello_sem, far_s,
):
    i = lax.axis_index("dp")
    j = lax.axis_index("tensor")
    c = lax.rem(i, 2)
    y = lax.rem(lax.div(i, 2), 4)
    z = lax.div(i, 8)
    x = lax.rem(j, 4)
    zh = lax.div(j, 4)
    oc = 1 - c

    def dev(z_=z, y_=y, c_=c, zh_=zh, x_=x):
        return ((z_ * 4 + y_) * 2 + c_, zh_ * 4 + x_)

    def remote(src, dst, ss, rs, to):
        return pltpu.make_async_remote_copy(
            src_ref=src, dst_ref=dst, send_sem=ss, recv_sem=rs,
            device_id=to, device_id_type=pl.DeviceIdType.MESH,
        )

    sib = dev(c_=oc)

    def ymod(k):
        return lax.rem(y + k, 4)

    def xmod(k):
        return lax.rem(x + k, 4)

    def zmod(k):
        return lax.rem(z + k, 8)

    def chunk(zz, yy):
        return w.at[lax.rem(zz, 4), :, lax.div(zz, 4), yy]

    def half(zz, yy, g):
        return w.at[lax.rem(zz, 4), g, lax.div(zz, 4), yy]

    loads = [
        pltpu.make_async_copy(gw_hbm, half(z, y, 0), loc_sem.at[0]),
        pltpu.make_async_copy(uw_hbm, half(z, y, 1), loc_sem.at[1]),
        pltpu.make_async_copy(hid_hbm, vin.at[0], loc_sem.at[2]),
        pltpu.make_async_copy(gate_hbm, vin.at[1], loc_sem.at[3]),
        pltpu.make_async_copy(up_hbm, vin.at[2], loc_sem.at[4]),
        pltpu.make_async_copy(tok_hbm, tok, loc_sem.at[5]),
    ]
    for load in loads:
        load.start()

    barrier = pltpu.get_barrier_semaphore()
    zf = zh * 8 + z

    def ring(k):
        to = lax.rem(zf + k, 16)
        return dev(z_=lax.rem(to, 8), zh_=lax.div(to, 8))

    partners = [sib] + [ring(k) for k in (1, 15, 2, 14)]
    partners += [dev(y_=ymod(k)) for k in range(1, 4)]
    partners += [dev(x_=xmod(k)) for k in range(1, 4)]
    for to in partners:
        pl.semaphore_signal(
            barrier, inc=1, device_id=to, device_id_type=pl.DeviceIdType.MESH
        )
    for load in loads[:2]:
        load.wait()

    def act_rows(r, _):
        rows = pl.ds(pl.multiple_of(r * 16, 16), 16)
        h32 = vin[0, rows, :].astype(F32)
        g32 = vin[1, rows, :].astype(F32)
        u32 = vin[2, rows, :].astype(F32)
        sig = jax.nn.sigmoid(g32)
        hs = h32 * sig
        acts[c, 0, rows, :] = (hs * u32 * (1.0 + g32 * (1.0 - sig))).astype(BF16)
        acts[c, 1, rows, :] = (hs * g32).astype(BF16)
        return 0

    def token_cov(k):
        own_tok = tok[:, pl.ds(pl.multiple_of(j * 128, 128), 128)]
        cols = tok[:, pl.ds(pl.multiple_of(k * 128, 128), 128)]
        covp[0, k] = lax.dot_general(own_tok, cols, TN, preferred_element_type=F32)

    def act_send(r):
        rows = pl.ds(pl.multiple_of(r * 64, 64), 64)
        piece = acts.at[c, :, rows]
        return remote(piece, piece, as_s.at[r], as_r.at[r], sib)

    def act_recv(r):
        rows = pl.ds(pl.multiple_of(r * 64, 64), 64)
        piece = acts.at[oc, :, rows]
        return remote(piece, piece, as_s.at[r], as_r.at[r], sib)

    def local_part(s):
        @pl.when(s < 4)
        def _():
            @pl.when(s == 0)
            def _():
                for load in loads[2:5]:
                    load.wait()

            def rows4(r, _):
                act_rows(s * 4 + r, 0)
                return 0

            lax.fori_loop(0, 4, rows4, 0)
            act_send(s).start()

        @pl.when((s >= 4) & (s < 8))
        def _():
            @pl.when(s == 4)
            def _():
                loads[5].wait()

            token_cov(s * 2 - 8)
            token_cov(s * 2 - 7)

            @pl.when(s == 7)
            def _():
                d0_send(0).start()

    pl.semaphore_wait(barrier, 11)

    def z_up(zz, g):
        return remote(
            half(zz, y, g), half(zz, y, g), zs_s.at[0, g, zz], z_r.at[g, zz], dev(z_=z + 1)
        )

    def z_dn(zz, g):
        return remote(
            half(zz, y, g), half(zz, y, g), zs_s.at[1, g, zz], z_r.at[g, zz], dev(z_=z - 1)
        )

    def y_send(zz, d, g):
        to = dev(y_=ymod(1 if d == 0 else 3))
        return remote(
            half(zz, y, g), half(zz, y, g), ys_s.at[d, g, zz], y_r.at[d, g, zz], to
        )

    def y_recv(zz, d, g):
        src = ymod(3 if d == 0 else 1)
        return remote(
            half(zz, src, g), half(zz, src, g), ys_s.at[d, g, zz], y_r.at[d, g, zz], sib
        )

    def y2_send(zz, d):
        src = ymod(3 if d == 0 else 1)
        to = dev(y_=ymod(1 if d == 0 else 3))
        return remote(half(zz, src, d), half(zz, src, d), y2s_s.at[d, zz], y2_r.at[d, zz], to)

    def y2_recv(zz, d):
        src = ymod(2)
        return remote(half(zz, src, d), half(zz, src, d), y2s_s.at[d, zz], y2_r.at[d, zz], sib)

    def each(s, fn):
        @pl.when((s >= 0) & (z - s >= 0) & (z - s <= 7))
        def _():
            fn(z - s, 0)

        @pl.when((s >= 1) & (z + s <= 7))
        def _():
            fn(z + s, 1)

    def arrive_z(s):
        def fn(zz, d):
            for g in range(2):
                @pl.when(s > 0)
                def _():
                    remote(
                        half(zz, y, g), half(zz, y, g), zs_s.at[0, g, zz], z_r.at[g, zz], sib
                    ).wait_recv()

                if d == 0:
                    @pl.when((z < 7) & (s < CHAIN))
                    def _():
                        z_up(zz, g).start()

                    @pl.when((s == 0) & (z > 0))
                    def _():
                        z_dn(zz, g).start()
                else:
                    @pl.when((z > 0) & (s < CHAIN))
                    def _():
                        z_dn(zz, g).start()
                y_send(zz, g, g).start()
                y_send(zz, 1 - g, g).start()
        return fn

    def arrive_y(zz, _):
        for d in range(2):
            y_recv(zz, d, d).wait_recv()
            y2_send(zz, d).start()

    def arrive_y2(zz, _):
        for d in range(2):
            y_recv(zz, d, 1 - d).wait_recv()
            y2_recv(zz, d).wait_recv()
        project(zz)

    def x_send(zz):
        to, hh = lax.rem(zz, 4), lax.div(zz, 4)
        return remote(xs.at[zz], xr.at[hh, x], xs_s.at[zz], xs_r.at[hh, x], dev(x_=to))

    def x_recv(k, hh):
        src = xmod(k)
        return remote(xs.at[src], xr.at[hh, src], xs_s.at[src], xs_r.at[hh, src], sib)

    def project(zz):
        t, hh = lax.rem(zz, 4), lax.div(zz, 4)
        wg = w[t, 0, hh].reshape(64, 1792)
        wu = w[t, 1, hh].reshape(64, 1792)
        for cc in range(2):
            part = lax.dot_general(wg, acts[cc, 0], NT, preferred_element_type=F32)
            part += lax.dot_general(wu, acts[cc, 1], NT, preferred_element_type=F32)

            @pl.when(t == x)
            def _():
                pown[hh, cc] = part

            @pl.when(t != x)
            def _():
                xs[zz, cc] = part.astype(BF16)

        @pl.when(t != x)
        def _():
            x_send(zz).start()

    def z8(hh):
        return remote(zsb.at[hh], zrb.at[hh], z8_s.at[hh], z8_r.at[hh], dev(zh_=1 - zh))


    def x_sum(hh):
        for k in range(1, 4):
            x_recv(k, hh).wait_recv()
        for cc in range(2):
            total = pown[hh, cc]
            for k in range(1, 4):
                total = total + xr[hh, xmod(k), cc].astype(F32)
            pown[hh, cc] = total
            zsb[hh, cc] = total.astype(BF16)
        z8(hh).start()

    def hello():
        for d, k in ((0, 2), (1, 14)):
            pl.semaphore_signal(
                hello_sem.at[d], inc=1, device_id=ring(k), device_id_type=pl.DeviceIdType.MESH
            )

    def far(d, k, g):
        to = dev(z_=z + k if d == 0 else z - k)
        return remote(half(z, y, g), half(z, y, g), far_s.at[d, g, k], z_r.at[g, z], to)

    def each_far(fn):
        for k in range(7, CHAIN, -1):
            @pl.when(z + k <= 7)
            def _():
                for g in range(2):
                    fn(far(0, k, g))

            @pl.when(z - k >= 0)
            def _():
                for g in range(2):
                    fn(far(1, k, g))

    def step(s, _):
        @pl.when(s < HELLOS)
        def _():
            hello()

        @pl.when(s == HELLOS)
        def _():
            each_far(lambda copy: copy.start())

        each(s, arrive_z(s))

        local_part(s)

        each(s - 1, arrive_y)

        @pl.when(s == LAG)
        def _():
            for r in range(4):
                act_recv(r).wait_recv()

        each(s - LAG, arrive_y2)

        def own_sum(hh, _):
            @pl.when(jnp.abs(z - x - 4 * hh) == s - LAG - 1)
            def _():
                x_sum(hh)
            return 0

        lax.fori_loop(0, 2, own_sum, 0)

        @pl.when(s < HELLOS)
        def _():
            for d in range(2):
                pl.semaphore_wait(hello_sem.at[d], 1)
        return 0

    def d0_send(m):
        rows = pl.ds(pl.multiple_of(oc * 64, 64), 64)
        return remote(covp.at[m, :, rows], d0r.at[m], d0_s.at[m], d0_r.at[m], sib)

    def d1_send(m, k):
        to = ymod(k)
        return remote(d1s.at[m, to], d1r.at[m, y], d1_s.at[m, to], d1_r.at[m, y], dev(y_=to))

    def d1_recv(m, k):
        src = ymod(k)
        return remote(d1s.at[m, src], d1r.at[m, src], d1_s.at[m, src], d1_r.at[m, src], sib)

    def d2_send(m, k):
        to = zmod(k)
        return remote(d2s.at[m, to], d2r.at[m, z], d2_s.at[m, to], d2_r.at[m, z], dev(z_=to))

    def d2_recv(m, k):
        src = zmod(k)
        return remote(d2s.at[m, src], d2r.at[m, src], d2_s.at[m, src], d2_r.at[m, src], sib)

    def d3_send(m, k):
        to = zmod(k)
        piece = fin.at[m, c, y, z]
        return remote(piece, piece, d3_s.at[m, to], d3_r.at[m, z], dev(z_=to))

    def d3_recv(m, k):
        src = zmod(k)
        piece = fin.at[m, c, y, src]
        return remote(piece, piece, d3_s.at[m, src], d3_r.at[m, src], sib)

    def d4_send(m, k):
        to = ymod(k)
        piece = fin.at[m, c, y]
        return remote(piece, piece, d4_s.at[m, to], d4_r.at[m, y], dev(y_=to))

    def d4_recv(m, k):
        src = ymod(k)
        piece = fin.at[m, c, src]
        return remote(piece, piece, d4_s.at[m, src], d4_r.at[m, src], sib)

    def d5_send(m):
        return remote(fin.at[m, c], fin.at[m, c], d5_s.at[m], d5_r.at[m], sib)

    def d5_recv(m):
        return remote(fin.at[m, oc], fin.at[m, oc], d5_s.at[m], d5_r.at[m], sib)

    def core_sum(m):
        d0_send(m).wait_recv()
        for yy in range(4):
            rows = pl.ds(pl.multiple_of(c * 64 + yy * 16, 16), 16)
            total = covp[m, :, rows, :] + d0r[m, :, yy * 16:(yy + 1) * 16, :]
            covp[m, :, rows, :] = total
            d1s[m, yy] = total.astype(BF16)
        for k in (2, 1, 3):
            d1_send(m, k).start()

    def y_sum(m):
        rows = pl.ds(pl.multiple_of(c * 64 + y * 16, 16), 16)
        total = covp[m, :, rows, :]
        for k in (1, 3, 2):
            d1_recv(m, k).wait_recv()
            total = total + d1r[m, ymod(k)].astype(F32)
        covp[m, :, rows, :] = total
        d2s[m] = total.astype(BF16)
        for k in range(1, 8):
            d2_send(m, k).start()

    def z_sum(m):
        rows = pl.ds(pl.multiple_of(c * 64 + y * 16, 16), 16)
        total = covp[m, z, rows, :]
        for k in range(1, 8):
            d2_recv(m, k).wait_recv()
            total = total + d2r[m, zmod(k)].astype(F32)
        fin[m, c, y, z] = (total * (1.0 / COUNT)).astype(BF16)
        for k in range(1, 8):
            d3_send(m, k).start()

    def z_back(m):
        for k in range(1, 8):
            d3_recv(m, k).wait_recv()
        for k in (2, 1, 3):
            d4_send(m, k).start()

    def y_back(m):
        for k in (1, 3, 2):
            d4_recv(m, k).wait_recv()
        d5_send(m).start()

    def put(m, cc):
        return pltpu.make_async_copy(fin.at[m, cc], fin_out.at[m, cc], out_sem.at[m, cc])

    lax.fori_loop(0, 9 + LAG, step, 0)

    core_sum(0)
    y_sum(0)

    def drain(zz, _):
        for g in range(2):
            @pl.when((z < 7) & (zz <= z) & (z - zz < CHAIN))
            def _():
                z_up(zz, g).wait_send()

            @pl.when((z > 0) & (zz >= z) & (zz - z < CHAIN))
            def _():
                z_dn(zz, g).wait_send()

            for d in range(2):
                y_send(zz, d, g).wait_send()
            y2_send(zz, g).wait_send()
        return 0


    def xg_send(k, cc, hh):
        to = xmod(k)
        return remote(
            gs.at[cc, hh], gt.at[hh, x, :, c], xg_s.at[to, cc, hh], xg_r.at[x, c, hh],
            dev(c_=cc, x_=to),
        )

    def xg_recv(k, cc, hh):
        src = xmod(k)
        return remote(
            gs.at[cc, hh], gt.at[hh, src, :, cc], xg_s.at[src, cc, hh], xg_r.at[src, cc, hh], sib
        )

    first = jnp.where(jnp.abs(z - x) <= jnp.abs(z - x - 4), 0, 1)
    for hh in (first, 1 - first):
        z8(hh).wait_recv()
        for cc in range(2):
            grad = (pown[hh, cc] + zrb[hh, cc].astype(F32)).astype(BF16)
            gs[cc, hh] = grad.reshape(4, 16, 256)
        xg_send(0, oc, hh).start()
        for k in (2, 1, 3):
            for cc in range(2):
                xg_send(k, cc, hh).start()
        mine = gs[c, hh]
        for yy in range(4):
            gt[hh, x, yy, c] = mine[yy]
    for hh in range(2):
        xg_recv(0, oc, hh).wait_recv()
    own = gt[zh, x].reshape(128, 256)
    own_out[...] = own

    def cov_cols(k):
        xx = xmod(k)
        for hh in range(2):
            covp[1, hh * 4 + xx] = lax.dot_general(
                own, gt[hh, xx].reshape(128, 256), NT, preferred_element_type=F32
            )

    cov_cols(0)
    z_sum(0)
    for k in (1, 3, 2):
        for cc in range(2):
            for hh in range(2):
                xg_recv(k, cc, hh).wait_recv()
        cov_cols(k)
    d0_send(1).start()

    def drain_sums(m):
        d0_send(m).wait_send()
        for k in range(1, 4):
            d1_send(m, k).wait_send()
        for k in range(1, 8):
            d2_send(m, k).wait_send()

    core_sum(1)
    y_sum(1)
    z_back(0)
    lax.fori_loop(0, 8, drain, 0)
    z_sum(1)
    y_back(0)
    put(0, c).start()
    each_far(lambda copy: copy.wait_send())
    for r in range(4):
        act_send(r).wait_send()
    for k in range(1, 4):
        for hh in range(2):
            x_send(xmod(k) + 4 * hh).wait_send()
    for hh in range(2):
        z8(hh).wait_send()
        xg_send(0, oc, hh).wait_send()
        for k in range(1, 4):
            for cc in range(2):
                xg_send(k, cc, hh).wait_send()
    drain_sums(0)
    z_back(1)
    d5_recv(0).wait_recv()
    put(0, oc).start()
    drain_sums(1)
    for m in range(2):
        for k in range(1, 8):
            d3_send(m, k).wait_send()
    y_back(1)
    put(1, c).start()
    for m in range(2):
        for k in range(1, 4):
            d4_send(m, k).wait_send()
    d5_send(0).wait_send()
    for cc in (c, oc):
        put(0, cc).wait()
    d5_recv(1).wait_recv()
    put(1, oc).start()
    d5_send(1).wait_send()
    for cc in (c, oc):
        put(1, cc).wait()


def arrange(fin, own, ig_out, act_out, cov_out):
    ig_out[...] = own[...].astype(F32).T.astype(BF16)
    for m, out in enumerate((act_out, cov_out)):
        for q in range(8):
            for k in range(8):
                out[q * 16:(q + 1) * 16, k * 128:(k + 1) * 128] = fin[m, q // 4, q % 4, k].astype(F32)


def shards(tokens, hidden_grad, gate, up, gate_weight, up_weight):
    sem = pltpu.SemaphoreType.DMA
    fin, own = pl.pallas_call(
        kernel,
        out_shape=(
            jax.ShapeDtypeStruct((2, 2, 4, 8, 16, 128), BF16),
            jax.ShapeDtypeStruct((128, 256), BF16),
        ),
        in_specs=[pl.BlockSpec(memory_space=pltpu.HBM)] * 6,
        out_specs=(
            pl.BlockSpec(memory_space=pl.ANY),
            pl.BlockSpec(memory_space=pltpu.VMEM),
        ),
        scratch_shapes=[
            pltpu.VMEM((256, 1024), BF16),
            pltpu.VMEM((3, 256, 1792), BF16),
            pltpu.VMEM((2, 2, 256, 1792), BF16),
            pltpu.VMEM((4, 2, 2, 4, 16, 1792), BF16),
            pltpu.VMEM((2, 2, 64, 256), F32),
            pltpu.VMEM((8, 2, 64, 256), BF16),
            pltpu.VMEM((2, 4, 2, 64, 256), BF16),
            pltpu.VMEM((2, 2, 64, 256), BF16),
            pltpu.VMEM((2, 2, 64, 256), BF16),
            pltpu.VMEM((2, 2, 4, 16, 256), BF16),
            pltpu.VMEM((2, 4, 4, 2, 16, 256), BF16),
            pltpu.VMEM((2, 8, 128, 128), F32),
            pltpu.VMEM((2, 8, 64, 128), F32),
            pltpu.VMEM((2, 4, 8, 16, 128), BF16),
            pltpu.VMEM((2, 4, 8, 16, 128), BF16),
            pltpu.VMEM((2, 8, 16, 128), BF16),
            pltpu.VMEM((2, 8, 16, 128), BF16),
            pltpu.VMEM((2, 2, 4, 8, 16, 128), BF16),
            sem((6,)), sem((4,)), sem((4,)),
            sem((2, 2, 8)), sem((2, 8)),
            sem((2, 2, 8)), sem((2, 2, 8)),
            sem((2, 8)), sem((2, 8)),
            sem((8,)), sem((2, 4)),
            sem((2,)), sem((2,)),
            sem((4, 2, 2)), sem((4, 2, 2)), sem((2, 2)),
            sem((2,)), sem((2,)),
            sem((2, 4)), sem((2, 4)),
            sem((2, 8)), sem((2, 8)),
            sem((2, 8)), sem((2, 8)),
            sem((2, 4)), sem((2, 4)),
            sem((2,)), sem((2,)),
            pltpu.SemaphoreType.REGULAR((2,)),
            sem((2, 2, 8)),
        ],
        compiler_params=pltpu.CompilerParams(
            collective_id=1, has_side_effects=True, vmem_limit_bytes=60 << 20
        ),
        cost_estimate=pl.CostEstimate(
            flops=2_500_000_000, bytes_accessed=10_000_000, transcendentals=1_000_000
        ),
        name="kfac_stats",
    )(tokens, hidden_grad, gate, up, gate_weight, up_weight)
    return tuple(
        pl.pallas_call(
            arrange,
            out_shape=(
                jax.ShapeDtypeStruct((256, 128), BF16),
                jax.ShapeDtypeStruct((128, 1024), F32),
                jax.ShapeDtypeStruct((128, 1024), F32),
            ),
            in_specs=[pl.BlockSpec(memory_space=pltpu.VMEM)] * 2,
            out_specs=tuple([pl.BlockSpec(memory_space=pltpu.VMEM)] * 3),
            compiler_params=pltpu.CompilerParams(vmem_limit_bytes=16 << 20),
            name="arrange",
        )(fin, own)
    )


def solution(mesh):
    placed = (
        P("dp", None),
        P("dp", "tensor"),
        P("dp", "tensor"),
        P("dp", "tensor"),
        P("dp", "tensor"),
        P("dp", "tensor"),
    )
    return jax.shard_map(
        shards,
        mesh=mesh,
        in_specs=placed,
        out_specs=(P("dp", "tensor"), P("tensor", None), P("tensor", None)),
        check_vma=False,
    )
```

```python
import jax
import jax.numpy as jnp
from jax import lax
from jax.experimental import pallas as pl
from jax.experimental.pallas import tpu as pltpu
from jax.sharding import PartitionSpec as P

BF16 = jnp.bfloat16
F32 = jnp.float32
NT = (((1,), (1,)), ((), ()))
TN = (((0,), (0,)), ((), ()))
COUNT = 16384
LAG, CHAIN, HELLOS = 3, 6, 3
STOP = 9


def kernel(
    tok_hbm, hid_hbm, gate_hbm, up_hbm, gw_hbm, uw_hbm,
    fin_out, own_out,
    tok, vin, acts, w, pown, xs, xr, zsb, zrb, gs, gt,
    covp, d0r, d1s, d1r, d2s, d2r, fin,
    loc_sem, as_s, as_r, zs_s, z_r, ys_s, y_r, y2s_s, y2_r,
    xs_s, xs_r, z8_s, z8_r, xg_s, xg_r, out_sem,
    d0_s, d0_r, d1_s, d1_r, d2_s, d2_r, d3_s, d3_r, d4_s, d4_r, d5_s, d5_r, hello_sem, far_s,
):
    i = lax.axis_index("dp")
    j = lax.axis_index("tensor")
    c = lax.rem(i, 2)
    y = lax.rem(lax.div(i, 2), 4)
    z = lax.div(i, 8)
    x = lax.rem(j, 4)
    zh = lax.div(j, 4)
    oc = 1 - c

    def dev(z_=z, y_=y, c_=c, zh_=zh, x_=x):
        return ((z_ * 4 + y_) * 2 + c_, zh_ * 4 + x_)

    def remote(src, dst, ss, rs, to):
        return pltpu.make_async_remote_copy(
            src_ref=src, dst_ref=dst, send_sem=ss, recv_sem=rs,
            device_id=to, device_id_type=pl.DeviceIdType.MESH,
        )

    sib = dev(c_=oc)

    def ymod(k):
        return lax.rem(y + k, 4)

    def xmod(k):
        return lax.rem(x + k, 4)

    def zmod(k):
        return lax.rem(z + k, 8)

    def chunk(zz, yy):
        return w.at[lax.rem(zz, 4), :, lax.div(zz, 4), yy]

    def half(zz, yy, g):
        return w.at[lax.rem(zz, 4), g, lax.div(zz, 4), yy]

    loads = [
        pltpu.make_async_copy(gw_hbm, half(z, y, 0), loc_sem.at[0]),
        pltpu.make_async_copy(uw_hbm, half(z, y, 1), loc_sem.at[1]),
        pltpu.make_async_copy(hid_hbm, vin.at[0], loc_sem.at[2]),
        pltpu.make_async_copy(gate_hbm, vin.at[1], loc_sem.at[3]),
        pltpu.make_async_copy(up_hbm, vin.at[2], loc_sem.at[4]),
        pltpu.make_async_copy(tok_hbm, tok, loc_sem.at[5]),
    ]
    for load in loads:
        load.start()

    barrier = pltpu.get_barrier_semaphore()
    zf = zh * 8 + z

    def ring(k):
        to = lax.rem(zf + k, 16)
        return dev(z_=lax.rem(to, 8), zh_=lax.div(to, 8))

    partners = [sib] + [ring(k) for k in (1, 15, 2, 14)]
    partners += [dev(y_=ymod(k)) for k in range(1, 4)]
    partners += [dev(x_=xmod(k)) for k in range(1, 4)]
    for to in partners:
        pl.semaphore_signal(
            barrier, inc=1, device_id=to, device_id_type=pl.DeviceIdType.MESH
        )
    for load in loads[:2]:
        load.wait()

    def act_rows(r, _):
        rows = pl.ds(pl.multiple_of(r * 16, 16), 16)
        h32 = vin[0, rows, :].astype(F32)
        g32 = vin[1, rows, :].astype(F32)
        u32 = vin[2, rows, :].astype(F32)
        sig = jax.nn.sigmoid(g32)
        hs = h32 * sig
        acts[c, 0, rows, :] = (hs * u32 * (1.0 + g32 * (1.0 - sig))).astype(BF16)
        acts[c, 1, rows, :] = (hs * g32).astype(BF16)
        return 0

    def token_cov(k):
        own_tok = tok[:, pl.ds(pl.multiple_of(j * 128, 128), 128)]
        cols = tok[:, pl.ds(pl.multiple_of(k * 128, 128), 128)]
        covp[0, k] = lax.dot_general(own_tok, cols, TN, preferred_element_type=F32)

    def act_send(r):
        rows = pl.ds(pl.multiple_of(r * 64, 64), 64)
        piece = acts.at[c, :, rows]
        return remote(piece, piece, as_s.at[r], as_r.at[r], sib)

    def act_recv(r):
        rows = pl.ds(pl.multiple_of(r * 64, 64), 64)
        piece = acts.at[oc, :, rows]
        return remote(piece, piece, as_s.at[r], as_r.at[r], sib)

    def local_part(s):
        @pl.when(s < 4)
        def _():
            @pl.when(s == 0)
            def _():
                for load in loads[2:5]:
                    load.wait()

            def rows4(r, _):
                act_rows(s * 4 + r, 0)
                return 0

            lax.fori_loop(0, 4, rows4, 0)
            act_send(s).start()

        @pl.when((s >= 4) & (s < 8))
        def _():
            @pl.when(s == 4)
            def _():
                loads[5].wait()

            token_cov(s * 2 - 8)
            token_cov(s * 2 - 7)

            @pl.when(s == 7)
            def _():
                d0_send(0).start()

    pl.semaphore_wait(barrier, 11)

    def z_up(zz, g):
        return remote(
            half(zz, y, g), half(zz, y, g), zs_s.at[0, g, zz], z_r.at[g, zz], dev(z_=z + 1)
        )

    def z_dn(zz, g):
        return remote(
            half(zz, y, g), half(zz, y, g), zs_s.at[1, g, zz], z_r.at[g, zz], dev(z_=z - 1)
        )

    def y_send(zz, d, g):
        to = dev(y_=ymod(1 if d == 0 else 3))
        return remote(
            half(zz, y, g), half(zz, y, g), ys_s.at[d, g, zz], y_r.at[d, g, zz], to
        )

    def y_recv(zz, d, g):
        src = ymod(3 if d == 0 else 1)
        return remote(
            half(zz, src, g), half(zz, src, g), ys_s.at[d, g, zz], y_r.at[d, g, zz], sib
        )

    def y2_send(zz, d):
        src = ymod(3 if d == 0 else 1)
        to = dev(y_=ymod(1 if d == 0 else 3))
        return remote(half(zz, src, d), half(zz, src, d), y2s_s.at[d, zz], y2_r.at[d, zz], to)

    def y2_recv(zz, d):
        src = ymod(2)
        return remote(half(zz, src, d), half(zz, src, d), y2s_s.at[d, zz], y2_r.at[d, zz], sib)

    def each(s, fn):
        @pl.when((s >= 0) & (z - s >= 0) & (z - s <= 7))
        def _():
            fn(z - s, 0)

        @pl.when((s >= 1) & (z + s <= 7))
        def _():
            fn(z + s, 1)

    def arrive_z(s):
        def fn(zz, d):
            for g in range(2):
                @pl.when(s > 0)
                def _():
                    remote(
                        half(zz, y, g), half(zz, y, g), zs_s.at[0, g, zz], z_r.at[g, zz], sib
                    ).wait_recv()

                if d == 0:
                    @pl.when((z < 7) & (s < CHAIN))
                    def _():
                        z_up(zz, g).start()

                    @pl.when((s == 0) & (z > 0))
                    def _():
                        z_dn(zz, g).start()
                else:
                    @pl.when((z > 0) & (s < CHAIN))
                    def _():
                        z_dn(zz, g).start()
                y_send(zz, g, g).start()
                y_send(zz, 1 - g, g).start()
        return fn

    def arrive_y(zz, _):
        for d in range(2):
            y_recv(zz, d, d).wait_recv()
            y2_send(zz, d).start()

    def arrive_y2(zz, _):
        for d in range(2):
            y_recv(zz, d, 1 - d).wait_recv()
            y2_recv(zz, d).wait_recv()
        project(zz)

    def x_send(zz):
        to, hh = lax.rem(zz, 4), lax.div(zz, 4)
        return remote(xs.at[zz], xr.at[hh, x], xs_s.at[zz], xs_r.at[hh, x], dev(x_=to))

    def x_recv(k, hh):
        src = xmod(k)
        return remote(xs.at[src], xr.at[hh, src], xs_s.at[src], xs_r.at[hh, src], sib)

    def project(zz):
        t, hh = lax.rem(zz, 4), lax.div(zz, 4)
        wg = w[t, 0, hh].reshape(64, 1792)
        wu = w[t, 1, hh].reshape(64, 1792)
        for cc in range(2):
            part = lax.dot_general(wg, acts[cc, 0], NT, preferred_element_type=F32)
            part += lax.dot_general(wu, acts[cc, 1], NT, preferred_element_type=F32)

            @pl.when(t == x)
            def _():
                pown[hh, cc] = part

            @pl.when(t != x)
            def _():
                xs[zz, cc] = part.astype(BF16)

        @pl.when(t != x)
        def _():
            x_send(zz).start()

    def z8(hh):
        return remote(zsb.at[hh], zrb.at[hh], z8_s.at[hh], z8_r.at[hh], dev(zh_=1 - zh))


    def x_sum(hh):
        for k in range(1, 4):
            x_recv(k, hh).wait_recv()
        for cc in range(2):
            total = pown[hh, cc]
            for k in range(1, 4):
                total = total + xr[hh, xmod(k), cc].astype(F32)
            pown[hh, cc] = total
            zsb[hh, cc] = total.astype(BF16)
        z8(hh).start()

    def hello():
        for d, k in ((0, 2), (1, 14)):
            pl.semaphore_signal(
                hello_sem.at[d], inc=1, device_id=ring(k), device_id_type=pl.DeviceIdType.MESH
            )

    def far(d, k, g):
        to = dev(z_=z + k if d == 0 else z - k)
        return remote(half(z, y, g), half(z, y, g), far_s.at[d, g, k], z_r.at[g, z], to)

    def each_far(fn):
        for k in range(7, CHAIN, -1):
            @pl.when(z + k <= 7)
            def _():
                for g in range(2):
                    fn(far(0, k, g))

            @pl.when(z - k >= 0)
            def _():
                for g in range(2):
                    fn(far(1, k, g))

    def step(s, _):
        @pl.when(s < HELLOS)
        def _():
            hello()

        @pl.when(s == HELLOS)
        def _():
            each_far(lambda copy: copy.start())

        each(s, arrive_z(s))

        local_part(s)


        @pl.when(s == LAG)
        def _():
            for r in range(4):
                act_recv(r).wait_recv()

        each(s - LAG, arrive_y2)
        each(s - 1, arrive_y)

        def own_sum(hh, _):
            @pl.when(jnp.abs(z - x - 4 * hh) == s - LAG - 1)
            def _():
                x_sum(hh)
            return 0

        lax.fori_loop(0, 2, own_sum, 0)

        @pl.when(s < HELLOS)
        def _():
            for d in range(2):
                pl.semaphore_wait(hello_sem.at[d], 1)
        return 0

    def d0_send(m):
        rows = pl.ds(pl.multiple_of(oc * 64, 64), 64)
        return remote(covp.at[m, :, rows], d0r.at[m], d0_s.at[m], d0_r.at[m], sib)

    def d1_send(m, k):
        to = ymod(k)
        return remote(d1s.at[m, to], d1r.at[m, y], d1_s.at[m, to], d1_r.at[m, y], dev(y_=to))

    def d1_recv(m, k):
        src = ymod(k)
        return remote(d1s.at[m, src], d1r.at[m, src], d1_s.at[m, src], d1_r.at[m, src], sib)

    def d2_send(m, k):
        to = zmod(k)
        return remote(d2s.at[m, to], d2r.at[m, z], d2_s.at[m, to], d2_r.at[m, z], dev(z_=to))

    def d2_recv(m, k):
        src = zmod(k)
        return remote(d2s.at[m, src], d2r.at[m, src], d2_s.at[m, src], d2_r.at[m, src], sib)

    def d3_send(m, k):
        to = zmod(k)
        piece = fin.at[m, c, y, z]
        return remote(piece, piece, d3_s.at[m, to], d3_r.at[m, z], dev(z_=to))

    def d3_recv(m, k):
        src = zmod(k)
        piece = fin.at[m, c, y, src]
        return remote(piece, piece, d3_s.at[m, src], d3_r.at[m, src], sib)

    def d4_send(m, k):
        to = ymod(k)
        piece = fin.at[m, c, y]
        return remote(piece, piece, d4_s.at[m, to], d4_r.at[m, y], dev(y_=to))

    def d4_recv(m, k):
        src = ymod(k)
        piece = fin.at[m, c, src]
        return remote(piece, piece, d4_s.at[m, src], d4_r.at[m, src], sib)

    def d5_send(m):
        return remote(fin.at[m, c], fin.at[m, c], d5_s.at[m], d5_r.at[m], sib)

    def d5_recv(m):
        return remote(fin.at[m, oc], fin.at[m, oc], d5_s.at[m], d5_r.at[m], sib)

    def core_sum(m):
        d0_send(m).wait_recv()
        for yy in range(4):
            rows = pl.ds(pl.multiple_of(c * 64 + yy * 16, 16), 16)
            total = covp[m, :, rows, :] + d0r[m, :, yy * 16:(yy + 1) * 16, :]
            covp[m, :, rows, :] = total
            d1s[m, yy] = total.astype(BF16)
        for k in (2, 1, 3):
            d1_send(m, k).start()

    def y_sum(m):
        rows = pl.ds(pl.multiple_of(c * 64 + y * 16, 16), 16)
        total = covp[m, :, rows, :]
        for k in (1, 3, 2):
            d1_recv(m, k).wait_recv()
            total = total + d1r[m, ymod(k)].astype(F32)
        covp[m, :, rows, :] = total
        d2s[m] = total.astype(BF16)
        for k in range(1, 8):
            d2_send(m, k).start()

    def z_sum(m):
        rows = pl.ds(pl.multiple_of(c * 64 + y * 16, 16), 16)
        total = covp[m, z, rows, :]
        for k in range(1, 8):
            d2_recv(m, k).wait_recv()
            total = total + d2r[m, zmod(k)].astype(F32)
        fin[m, c, y, z] = (total * (1.0 / COUNT)).astype(BF16)
        for k in range(1, 8):
            d3_send(m, k).start()

    def z_back(m):
        for k in range(1, 8):
            d3_recv(m, k).wait_recv()
        for k in (2, 1, 3):
            d4_send(m, k).start()

    def y_back(m):
        for k in (1, 3, 2):
            d4_recv(m, k).wait_recv()
        d5_send(m).start()

    def put(m, cc):
        return pltpu.make_async_copy(fin.at[m, cc], fin_out.at[m, cc], out_sem.at[m, cc])

    lax.fori_loop(0, 9 + LAG, step, 0)

    core_sum(0)
    y_sum(0)

    def drain(zz, _):
        for g in range(2):
            @pl.when((z < 7) & (zz <= z) & (z - zz < CHAIN))
            def _():
                z_up(zz, g).wait_send()

            @pl.when((z > 0) & (zz >= z) & (zz - z < CHAIN))
            def _():
                z_dn(zz, g).wait_send()

            for d in range(2):
                y_send(zz, d, g).wait_send()
            y2_send(zz, g).wait_send()
        return 0


    def xg_send(k, cc, hh):
        to = xmod(k)
        return remote(
            gs.at[cc, hh], gt.at[hh, x, :, c], xg_s.at[to, cc, hh], xg_r.at[x, c, hh],
            dev(c_=cc, x_=to),
        )

    def xg_recv(k, cc, hh):
        src = xmod(k)
        return remote(
            gs.at[cc, hh], gt.at[hh, src, :, cc], xg_s.at[src, cc, hh], xg_r.at[src, cc, hh], sib
        )

    first = jnp.where(jnp.abs(z - x) <= jnp.abs(z - x - 4), 0, 1)
    for hh in (first, 1 - first):
        z8(hh).wait_recv()
        for cc in range(2):
            grad = (pown[hh, cc] + zrb[hh, cc].astype(F32)).astype(BF16)
            gs[cc, hh] = grad.reshape(4, 16, 256)
        xg_send(0, oc, hh).start()
        for k in (2, 1, 3):
            for cc in range(2):
                xg_send(k, cc, hh).start()
        mine = gs[c, hh]
        for yy in range(4):
            gt[hh, x, yy, c] = mine[yy]
    for hh in range(2):
        xg_recv(0, oc, hh).wait_recv()
    own = gt[zh, x].reshape(128, 256)
    own_out[...] = own

    def cov_cols(k):
        xx = xmod(k)
        for hh in range(2):
            covp[1, hh * 4 + xx] = lax.dot_general(
                own, gt[hh, xx].reshape(128, 256), NT, preferred_element_type=F32
            )

    cov_cols(0)
    z_sum(0)
    for k in (1, 3, 2):
        for cc in range(2):
            for hh in range(2):
                xg_recv(k, cc, hh).wait_recv()
        cov_cols(k)
    d0_send(1).start()

    def drain_sums(m):
        d0_send(m).wait_send()
        for k in range(1, 4):
            d1_send(m, k).wait_send()
        for k in range(1, 8):
            d2_send(m, k).wait_send()

    core_sum(1)
    y_sum(1)
    z_back(0)
    lax.fori_loop(0, 8, drain, 0)
    z_sum(1)
    y_back(0)
    put(0, c).start()
    each_far(lambda copy: copy.wait_send())
    for r in range(4):
        act_send(r).wait_send()
    for k in range(1, 4):
        for hh in range(2):
            x_send(xmod(k) + 4 * hh).wait_send()
    for hh in range(2):
        z8(hh).wait_send()
        xg_send(0, oc, hh).wait_send()
        for k in range(1, 4):
            for cc in range(2):
                xg_send(k, cc, hh).wait_send()
    drain_sums(0)
    z_back(1)
    d5_recv(0).wait_recv()
    put(0, oc).start()
    drain_sums(1)
    for m in range(2):
        for k in range(1, 8):
            d3_send(m, k).wait_send()
    y_back(1)
    put(1, c).start()
    for m in range(2):
        for k in range(1, 4):
            d4_send(m, k).wait_send()
    d5_send(0).wait_send()
    for cc in (c, oc):
        put(0, cc).wait()
    d5_recv(1).wait_recv()
    put(1, oc).start()
    d5_send(1).wait_send()
    for cc in (c, oc):
        put(1, cc).wait()


def arrange(fin, own, ig_out, act_out, cov_out):
    ig_out[...] = own[...].astype(F32).T.astype(BF16)
    for m, out in enumerate((act_out, cov_out)):
        for q in range(8):
            for k in range(8):
                out[q * 16:(q + 1) * 16, k * 128:(k + 1) * 128] = fin[m, q // 4, q % 4, k].astype(F32)


def shards(tokens, hidden_grad, gate, up, gate_weight, up_weight):
    sem = pltpu.SemaphoreType.DMA
    fin, own = pl.pallas_call(
        kernel,
        out_shape=(
            jax.ShapeDtypeStruct((2, 2, 4, 8, 16, 128), BF16),
            jax.ShapeDtypeStruct((128, 256), BF16),
        ),
        in_specs=[pl.BlockSpec(memory_space=pltpu.HBM)] * 6,
        out_specs=(
            pl.BlockSpec(memory_space=pl.ANY),
            pl.BlockSpec(memory_space=pltpu.VMEM),
        ),
        scratch_shapes=[
            pltpu.VMEM((256, 1024), BF16),
            pltpu.VMEM((3, 256, 1792), BF16),
            pltpu.VMEM((2, 2, 256, 1792), BF16),
            pltpu.VMEM((4, 2, 2, 4, 16, 1792), BF16),
            pltpu.VMEM((2, 2, 64, 256), F32),
            pltpu.VMEM((8, 2, 64, 256), BF16),
            pltpu.VMEM((2, 4, 2, 64, 256), BF16),
            pltpu.VMEM((2, 2, 64, 256), BF16),
            pltpu.VMEM((2, 2, 64, 256), BF16),
            pltpu.VMEM((2, 2, 4, 16, 256), BF16),
            pltpu.VMEM((2, 4, 4, 2, 16, 256), BF16),
            pltpu.VMEM((2, 8, 128, 128), F32),
            pltpu.VMEM((2, 8, 64, 128), F32),
            pltpu.VMEM((2, 4, 8, 16, 128), BF16),
            pltpu.VMEM((2, 4, 8, 16, 128), BF16),
            pltpu.VMEM((2, 8, 16, 128), BF16),
            pltpu.VMEM((2, 8, 16, 128), BF16),
            pltpu.VMEM((2, 2, 4, 8, 16, 128), BF16),
            sem((6,)), sem((4,)), sem((4,)),
            sem((2, 2, 8)), sem((2, 8)),
            sem((2, 2, 8)), sem((2, 2, 8)),
            sem((2, 8)), sem((2, 8)),
            sem((8,)), sem((2, 4)),
            sem((2,)), sem((2,)),
            sem((4, 2, 2)), sem((4, 2, 2)), sem((2, 2)),
            sem((2,)), sem((2,)),
            sem((2, 4)), sem((2, 4)),
            sem((2, 8)), sem((2, 8)),
            sem((2, 8)), sem((2, 8)),
            sem((2, 4)), sem((2, 4)),
            sem((2,)), sem((2,)),
            pltpu.SemaphoreType.REGULAR((2,)),
            sem((2, 2, 8)),
        ],
        compiler_params=pltpu.CompilerParams(
            collective_id=1, has_side_effects=True, vmem_limit_bytes=60 << 20
        ),
        cost_estimate=pl.CostEstimate(
            flops=2_500_000_000, bytes_accessed=10_000_000, transcendentals=1_000_000
        ),
        name="kfac_stats",
    )(tokens, hidden_grad, gate, up, gate_weight, up_weight)
    return tuple(
        pl.pallas_call(
            arrange,
            out_shape=(
                jax.ShapeDtypeStruct((256, 128), BF16),
                jax.ShapeDtypeStruct((128, 1024), F32),
                jax.ShapeDtypeStruct((128, 1024), F32),
            ),
            in_specs=[pl.BlockSpec(memory_space=pltpu.VMEM)] * 2,
            out_specs=tuple([pl.BlockSpec(memory_space=pltpu.VMEM)] * 3),
            compiler_params=pltpu.CompilerParams(vmem_limit_bytes=16 << 20),
            name="arrange",
        )(fin, own)
    )


def solution(mesh):
    placed = (
        P("dp", None),
        P("dp", "tensor"),
        P("dp", "tensor"),
        P("dp", "tensor"),
        P("dp", "tensor"),
        P("dp", "tensor"),
    )
    return jax.shard_map(
        shards,
        mesh=mesh,
        in_specs=placed,
        out_specs=(P("dp", "tensor"), P("tensor", None), P("tensor", None)),
        check_vma=False,
    )
```

```python
import jax
import jax.numpy as jnp
from jax import lax
from jax.experimental import pallas as pl
from jax.experimental.pallas import tpu as pltpu
from jax.sharding import PartitionSpec as P

BF16 = jnp.bfloat16
F32 = jnp.float32
NT = (((1,), (1,)), ((), ()))
TN = (((0,), (0,)), ((), ()))
COUNT = 16384
LAG, CHAIN, HELLOS = 3, 6, 3
STOP = 9


def kernel(
    tok_hbm, hid_hbm, gate_hbm, up_hbm, gw_hbm, uw_hbm,
    fin_out, own_out,
    tok, vin, acts, w, pown, xs, xr, zsb, zrb, gs, gt,
    covp, d0r, d1s, d1r, d2s, d2r, fin,
    loc_sem, as_s, as_r, zs_s, z_r, ys_s, y_r, y2s_s, y2_r,
    xs_s, xs_r, z8_s, z8_r, xg_s, xg_r, out_sem,
    d0_s, d0_r, d1_s, d1_r, d2_s, d2_r, d3_s, d3_r, d4_s, d4_r, d5_s, d5_r, hello_sem, far_s,
):
    i = lax.axis_index("dp")
    j = lax.axis_index("tensor")
    c = lax.rem(i, 2)
    y = lax.rem(lax.div(i, 2), 4)
    z = lax.div(i, 8)
    x = lax.rem(j, 4)
    zh = lax.div(j, 4)
    oc = 1 - c

    def dev(z_=z, y_=y, c_=c, zh_=zh, x_=x):
        return ((z_ * 4 + y_) * 2 + c_, zh_ * 4 + x_)

    def remote(src, dst, ss, rs, to):
        return pltpu.make_async_remote_copy(
            src_ref=src, dst_ref=dst, send_sem=ss, recv_sem=rs,
            device_id=to, device_id_type=pl.DeviceIdType.MESH,
        )

    sib = dev(c_=oc)

    def ymod(k):
        return lax.rem(y + k, 4)

    def xmod(k):
        return lax.rem(x + k, 4)

    def zmod(k):
        return lax.rem(z + k, 8)

    def chunk(zz, yy):
        return w.at[lax.rem(zz, 4), :, lax.div(zz, 4), yy]

    def half(zz, yy, g):
        return w.at[lax.rem(zz, 4), g, lax.div(zz, 4), yy]

    loads = [
        pltpu.make_async_copy(gw_hbm, half(z, y, 0), loc_sem.at[0]),
        pltpu.make_async_copy(uw_hbm, half(z, y, 1), loc_sem.at[1]),
        pltpu.make_async_copy(hid_hbm, vin.at[0], loc_sem.at[2]),
        pltpu.make_async_copy(gate_hbm, vin.at[1], loc_sem.at[3]),
        pltpu.make_async_copy(up_hbm, vin.at[2], loc_sem.at[4]),
        pltpu.make_async_copy(tok_hbm, tok, loc_sem.at[5]),
    ]
    for load in loads:
        load.start()

    barrier = pltpu.get_barrier_semaphore()
    zf = zh * 8 + z

    def ring(k):
        to = lax.rem(zf + k, 16)
        return dev(z_=lax.rem(to, 8), zh_=lax.div(to, 8))

    partners = [sib] + [ring(k) for k in (1, 15, 2, 14)]
    partners += [dev(y_=ymod(k)) for k in range(1, 4)]
    partners += [dev(x_=xmod(k)) for k in range(1, 4)]
    for to in partners:
        pl.semaphore_signal(
            barrier, inc=1, device_id=to, device_id_type=pl.DeviceIdType.MESH
        )
    for load in loads[:2]:
        load.wait()

    def act_rows(r, _):
        rows = pl.ds(pl.multiple_of(r * 16, 16), 16)
        h32 = vin[0, rows, :].astype(F32)
        g32 = vin[1, rows, :].astype(F32)
        u32 = vin[2, rows, :].astype(F32)
        sig = jax.nn.sigmoid(g32)
        hs = h32 * sig
        acts[c, 0, rows, :] = (hs * u32 * (1.0 + g32 * (1.0 - sig))).astype(BF16)
        acts[c, 1, rows, :] = (hs * g32).astype(BF16)
        return 0

    def token_cov(k):
        own_tok = tok[:, pl.ds(pl.multiple_of(j * 128, 128), 128)]
        cols = tok[:, pl.ds(pl.multiple_of(k * 128, 128), 128)]
        covp[0, lax.div(k, 4), lax.rem(k, 4)] = lax.dot_general(
            own_tok, cols, TN, preferred_element_type=F32
        )

    def act_send(r):
        rows = pl.ds(pl.multiple_of(r * 64, 64), 64)
        piece = acts.at[c, :, rows]
        return remote(piece, piece, as_s.at[r], as_r.at[r], sib)

    def act_recv(r):
        rows = pl.ds(pl.multiple_of(r * 64, 64), 64)
        piece = acts.at[oc, :, rows]
        return remote(piece, piece, as_s.at[r], as_r.at[r], sib)

    def local_part(s):
        @pl.when(s < 4)
        def _():
            @pl.when(s == 0)
            def _():
                for load in loads[2:5]:
                    load.wait()

            def rows4(r, _):
                act_rows(s * 4 + r, 0)
                return 0

            lax.fori_loop(0, 4, rows4, 0)
            act_send(s).start()

        @pl.when((s >= 4) & (s < 8))
        def _():
            @pl.when(s == 4)
            def _():
                loads[5].wait()

            token_cov(s * 2 - 8)
            token_cov(s * 2 - 7)

            @pl.when(s == 7)
            def _():
                for k in range(4):
                    d0_send(0, k).start()

    pl.semaphore_wait(barrier, 11)

    def z_up(zz, g):
        return remote(
            half(zz, y, g), half(zz, y, g), zs_s.at[0, g, zz], z_r.at[g, zz], dev(z_=z + 1)
        )

    def z_dn(zz, g):
        return remote(
            half(zz, y, g), half(zz, y, g), zs_s.at[1, g, zz], z_r.at[g, zz], dev(z_=z - 1)
        )

    def y_send(zz, d, g):
        to = dev(y_=ymod(1 if d == 0 else 3))
        return remote(
            half(zz, y, g), half(zz, y, g), ys_s.at[d, g, zz], y_r.at[d, g, zz], to
        )

    def y_recv(zz, d, g):
        src = ymod(3 if d == 0 else 1)
        return remote(
            half(zz, src, g), half(zz, src, g), ys_s.at[d, g, zz], y_r.at[d, g, zz], sib
        )

    def y2_send(zz, d):
        src = ymod(3 if d == 0 else 1)
        to = dev(y_=ymod(1 if d == 0 else 3))
        return remote(half(zz, src, d), half(zz, src, d), y2s_s.at[d, zz], y2_r.at[d, zz], to)

    def y2_recv(zz, d):
        src = ymod(2)
        return remote(half(zz, src, d), half(zz, src, d), y2s_s.at[d, zz], y2_r.at[d, zz], sib)

    def each(s, fn):
        @pl.when((s >= 0) & (z - s >= 0) & (z - s <= 7))
        def _():
            fn(z - s, 0)

        @pl.when((s >= 1) & (z + s <= 7))
        def _():
            fn(z + s, 1)

    def arrive_z(s):
        def fn(zz, d):
            for g in range(2):
                @pl.when(s > 0)
                def _():
                    remote(
                        half(zz, y, g), half(zz, y, g), zs_s.at[0, g, zz], z_r.at[g, zz], sib
                    ).wait_recv()

                if d == 0:
                    @pl.when((z < 7) & (s < CHAIN))
                    def _():
                        z_up(zz, g).start()

                    @pl.when((s == 0) & (z > 0))
                    def _():
                        z_dn(zz, g).start()
                else:
                    @pl.when((z > 0) & (s < CHAIN))
                    def _():
                        z_dn(zz, g).start()
                y_send(zz, g, g).start()
                y_send(zz, 1 - g, g).start()
        return fn

    def arrive_y(zz, _):
        for d in range(2):
            y_recv(zz, d, d).wait_recv()
            y2_send(zz, d).start()

    def arrive_y2(zz, _):
        for d in range(2):
            y_recv(zz, d, 1 - d).wait_recv()
            y2_recv(zz, d).wait_recv()
        project(zz)

    def x_send(zz):
        to, hh = lax.rem(zz, 4), lax.div(zz, 4)
        return remote(xs.at[zz], xr.at[hh, x], xs_s.at[zz], xs_r.at[hh, x], dev(x_=to))

    def x_recv(k, hh):
        src = xmod(k)
        return remote(xs.at[src], xr.at[hh, src], xs_s.at[src], xs_r.at[hh, src], sib)

    def project(zz):
        t, hh = lax.rem(zz, 4), lax.div(zz, 4)
        wg = w[t, 0, hh].reshape(64, 1792)
        wu = w[t, 1, hh].reshape(64, 1792)
        for cc in range(2):
            part = lax.dot_general(wg, acts[cc, 0], NT, preferred_element_type=F32)
            part += lax.dot_general(wu, acts[cc, 1], NT, preferred_element_type=F32)

            @pl.when(t == x)
            def _():
                pown[hh, cc] = part

            @pl.when(t != x)
            def _():
                xs[zz, cc] = part.astype(BF16)

        @pl.when(t != x)
        def _():
            x_send(zz).start()

    def z8(hh):
        return remote(zsb.at[hh], zrb.at[hh], z8_s.at[hh], z8_r.at[hh], dev(zh_=1 - zh))


    def x_sum(hh):
        for k in range(1, 4):
            x_recv(k, hh).wait_recv()
        for cc in range(2):
            total = pown[hh, cc]
            for k in range(1, 4):
                total = total + xr[hh, xmod(k), cc].astype(F32)
            pown[hh, cc] = total
            zsb[hh, cc] = total.astype(BF16)
        z8(hh).start()

    def hello():
        for d, k in ((0, 2), (1, 14)):
            pl.semaphore_signal(
                hello_sem.at[d], inc=1, device_id=ring(k), device_id_type=pl.DeviceIdType.MESH
            )

    def far(d, k, g):
        to = dev(z_=z + k if d == 0 else z - k)
        return remote(half(z, y, g), half(z, y, g), far_s.at[d, g, k], z_r.at[g, z], to)

    def each_far(fn):
        for k in range(7, CHAIN, -1):
            @pl.when(z + k <= 7)
            def _():
                for g in range(2):
                    fn(far(0, k, g))

            @pl.when(z - k >= 0)
            def _():
                for g in range(2):
                    fn(far(1, k, g))

    def step(s, _):
        @pl.when(s < HELLOS)
        def _():
            hello()

        @pl.when(s == HELLOS)
        def _():
            each_far(lambda copy: copy.start())

        each(s, arrive_z(s))

        local_part(s)


        @pl.when(s == LAG)
        def _():
            for r in range(4):
                act_recv(r).wait_recv()

        each(s - LAG, arrive_y2)
        each(s - 1, arrive_y)

        def own_sum(hh, _):
            @pl.when(jnp.abs(z - x - 4 * hh) == s - LAG - 1)
            def _():
                x_sum(hh)
            return 0

        lax.fori_loop(0, 2, own_sum, 0)

        @pl.when(s < HELLOS)
        def _():
            for d in range(2):
                pl.semaphore_wait(hello_sem.at[d], 1)
        return 0

    def d0_send(m, k):
        xx = xmod(k)
        rows = pl.ds(pl.multiple_of(oc * 64, 64), 64)
        return remote(
            covp.at[m, :, xx, rows], d0r.at[m, :, xx], d0_s.at[m, xx], d0_r.at[m, xx], sib
        )

    def d1_send(m, k):
        to = ymod(k)
        return remote(d1s.at[m, to], d1r.at[m, y], d1_s.at[m, to], d1_r.at[m, y], dev(y_=to))

    def d1_recv(m, k):
        src = ymod(k)
        return remote(d1s.at[m, src], d1r.at[m, src], d1_s.at[m, src], d1_r.at[m, src], sib)

    def d2_send(m, k):
        to = zmod(k)
        return remote(d2s.at[m, to], d2r.at[m, z], d2_s.at[m, to], d2_r.at[m, z], dev(z_=to))

    def d2_recv(m, k):
        src = zmod(k)
        return remote(d2s.at[m, src], d2r.at[m, src], d2_s.at[m, src], d2_r.at[m, src], sib)

    def d3_send(m, k):
        to = zmod(k)
        piece = fin.at[m, c, y, z]
        return remote(piece, piece, d3_s.at[m, to], d3_r.at[m, z], dev(z_=to))

    def d3_recv(m, k):
        src = zmod(k)
        piece = fin.at[m, c, y, src]
        return remote(piece, piece, d3_s.at[m, src], d3_r.at[m, src], sib)

    def d4_send(m, k):
        to = ymod(k)
        piece = fin.at[m, c, y]
        return remote(piece, piece, d4_s.at[m, to], d4_r.at[m, y], dev(y_=to))

    def d4_recv(m, k):
        src = ymod(k)
        piece = fin.at[m, c, src]
        return remote(piece, piece, d4_s.at[m, src], d4_r.at[m, src], sib)

    def d5_send(m):
        return remote(fin.at[m, c], fin.at[m, c], d5_s.at[m], d5_r.at[m], sib)

    def d5_recv(m):
        return remote(fin.at[m, oc], fin.at[m, oc], d5_s.at[m], d5_r.at[m], sib)

    def core_sum(m):
        for k in range(4):
            d0_send(m, k).wait_recv()
        for yy in range(4):
            rows = pl.ds(pl.multiple_of(c * 64 + yy * 16, 16), 16)
            total = covp[m, :, :, rows, :] + d0r[m, :, :, yy * 16:(yy + 1) * 16, :]
            covp[m, :, :, rows, :] = total
            d1s[m, yy] = total.reshape(8, 16, 128).astype(BF16)
        for k in (2, 1, 3):
            d1_send(m, k).start()

    def y_sum(m):
        rows = pl.ds(pl.multiple_of(c * 64 + y * 16, 16), 16)
        total = covp[m, :, :, rows, :].reshape(8, 16, 128)
        for k in (1, 3, 2):
            d1_recv(m, k).wait_recv()
            total = total + d1r[m, ymod(k)].astype(F32)
        covp[m, :, :, rows, :] = total.reshape(2, 4, 16, 128)
        d2s[m] = total.astype(BF16)
        for k in range(1, 8):
            d2_send(m, k).start()

    def z_sum(m):
        rows = pl.ds(pl.multiple_of(c * 64 + y * 16, 16), 16)
        total = covp[m, lax.div(z, 4), lax.rem(z, 4), rows, :]
        for k in range(1, 8):
            d2_recv(m, k).wait_recv()
            total = total + d2r[m, zmod(k)].astype(F32)
        fin[m, c, y, z] = (total * (1.0 / COUNT)).astype(BF16)
        for k in range(1, 8):
            d3_send(m, k).start()

    def z_back(m):
        for k in range(1, 8):
            d3_recv(m, k).wait_recv()
        for k in (2, 1, 3):
            d4_send(m, k).start()

    def y_back(m):
        for k in (1, 3, 2):
            d4_recv(m, k).wait_recv()
        d5_send(m).start()

    def put(m, cc):
        return pltpu.make_async_copy(fin.at[m, cc], fin_out.at[m, cc], out_sem.at[m, cc])

    lax.fori_loop(0, 9 + LAG, step, 0)

    core_sum(0)
    y_sum(0)

    def drain(zz, _):
        for g in range(2):
            @pl.when((z < 7) & (zz <= z) & (z - zz < CHAIN))
            def _():
                z_up(zz, g).wait_send()

            @pl.when((z > 0) & (zz >= z) & (zz - z < CHAIN))
            def _():
                z_dn(zz, g).wait_send()

            for d in range(2):
                y_send(zz, d, g).wait_send()
            y2_send(zz, g).wait_send()
        return 0


    def xg_send(k, cc, hh):
        to = xmod(k)
        return remote(
            gs.at[cc, hh], gt.at[hh, x, :, c], xg_s.at[to, cc, hh], xg_r.at[x, c, hh],
            dev(c_=cc, x_=to),
        )

    def xg_recv(k, cc, hh):
        src = xmod(k)
        return remote(
            gs.at[cc, hh], gt.at[hh, src, :, cc], xg_s.at[src, cc, hh], xg_r.at[src, cc, hh], sib
        )

    first = jnp.where(jnp.abs(z - x) <= jnp.abs(z - x - 4), 0, 1)
    for hh in (first, 1 - first):
        z8(hh).wait_recv()
        for cc in range(2):
            grad = (pown[hh, cc] + zrb[hh, cc].astype(F32)).astype(BF16)
            gs[cc, hh] = grad.reshape(4, 16, 256)
        xg_send(0, oc, hh).start()
        for k in (2, 1, 3):
            for cc in range(2):
                xg_send(k, cc, hh).start()
        mine = gs[c, hh]
        for yy in range(4):
            gt[hh, x, yy, c] = mine[yy]
    for hh in range(2):
        xg_recv(0, oc, hh).wait_recv()
    own = gt[zh, x].reshape(128, 256)
    own_out[...] = own

    def cov_cols(k):
        xx = xmod(k)
        for hh in range(2):
            covp[1, hh, xx] = lax.dot_general(
                own, gt[hh, xx].reshape(128, 256), NT, preferred_element_type=F32
            )

    cov_cols(0)
    d0_send(1, 0).start()
    z_sum(0)
    for k in (1, 3, 2):
        for cc in range(2):
            for hh in range(2):
                xg_recv(k, cc, hh).wait_recv()
        cov_cols(k)
        d0_send(1, k).start()

    def drain_sums(m):
        for k in range(4):
            d0_send(m, k).wait_send()
        for k in range(1, 4):
            d1_send(m, k).wait_send()
        for k in range(1, 8):
            d2_send(m, k).wait_send()

    core_sum(1)
    y_sum(1)
    z_back(0)
    lax.fori_loop(0, 8, drain, 0)
    z_sum(1)
    y_back(0)
    put(0, c).start()
    each_far(lambda copy: copy.wait_send())
    for r in range(4):
        act_send(r).wait_send()
    for k in range(1, 4):
        for hh in range(2):
            x_send(xmod(k) + 4 * hh).wait_send()
    for hh in range(2):
        z8(hh).wait_send()
        xg_send(0, oc, hh).wait_send()
        for k in range(1, 4):
            for cc in range(2):
                xg_send(k, cc, hh).wait_send()
    drain_sums(0)
    z_back(1)
    d5_recv(0).wait_recv()
    put(0, oc).start()
    drain_sums(1)
    for m in range(2):
        for k in range(1, 8):
            d3_send(m, k).wait_send()
    y_back(1)
    put(1, c).start()
    for m in range(2):
        for k in range(1, 4):
            d4_send(m, k).wait_send()
    d5_send(0).wait_send()
    for cc in (c, oc):
        put(0, cc).wait()
    d5_recv(1).wait_recv()
    put(1, oc).start()
    d5_send(1).wait_send()
    for cc in (c, oc):
        put(1, cc).wait()


def arrange(fin, own, ig_out, act_out, cov_out):
    ig_out[...] = own[...].astype(F32).T.astype(BF16)
    for m, out in enumerate((act_out, cov_out)):
        for q in range(8):
            for k in range(8):
                out[q * 16:(q + 1) * 16, k * 128:(k + 1) * 128] = fin[m, q // 4, q % 4, k].astype(F32)


def shards(tokens, hidden_grad, gate, up, gate_weight, up_weight):
    sem = pltpu.SemaphoreType.DMA
    fin, own = pl.pallas_call(
        kernel,
        out_shape=(
            jax.ShapeDtypeStruct((2, 2, 4, 8, 16, 128), BF16),
            jax.ShapeDtypeStruct((128, 256), BF16),
        ),
        in_specs=[pl.BlockSpec(memory_space=pltpu.HBM)] * 6,
        out_specs=(
            pl.BlockSpec(memory_space=pl.ANY),
            pl.BlockSpec(memory_space=pltpu.VMEM),
        ),
        scratch_shapes=[
            pltpu.VMEM((256, 1024), BF16),
            pltpu.VMEM((3, 256, 1792), BF16),
            pltpu.VMEM((2, 2, 256, 1792), BF16),
            pltpu.VMEM((4, 2, 2, 4, 16, 1792), BF16),
            pltpu.VMEM((2, 2, 64, 256), F32),
            pltpu.VMEM((8, 2, 64, 256), BF16),
            pltpu.VMEM((2, 4, 2, 64, 256), BF16),
            pltpu.VMEM((2, 2, 64, 256), BF16),
            pltpu.VMEM((2, 2, 64, 256), BF16),
            pltpu.VMEM((2, 2, 4, 16, 256), BF16),
            pltpu.VMEM((2, 4, 4, 2, 16, 256), BF16),
            pltpu.VMEM((2, 2, 4, 128, 128), F32),
            pltpu.VMEM((2, 2, 4, 64, 128), F32),
            pltpu.VMEM((2, 4, 8, 16, 128), BF16),
            pltpu.VMEM((2, 4, 8, 16, 128), BF16),
            pltpu.VMEM((2, 8, 16, 128), BF16),
            pltpu.VMEM((2, 8, 16, 128), BF16),
            pltpu.VMEM((2, 2, 4, 8, 16, 128), BF16),
            sem((6,)), sem((4,)), sem((4,)),
            sem((2, 2, 8)), sem((2, 8)),
            sem((2, 2, 8)), sem((2, 2, 8)),
            sem((2, 8)), sem((2, 8)),
            sem((8,)), sem((2, 4)),
            sem((2,)), sem((2,)),
            sem((4, 2, 2)), sem((4, 2, 2)), sem((2, 2)),
            sem((2, 4)), sem((2, 4)),
            sem((2, 4)), sem((2, 4)),
            sem((2, 8)), sem((2, 8)),
            sem((2, 8)), sem((2, 8)),
            sem((2, 4)), sem((2, 4)),
            sem((2,)), sem((2,)),
            pltpu.SemaphoreType.REGULAR((2,)),
            sem((2, 2, 8)),
        ],
        compiler_params=pltpu.CompilerParams(
            collective_id=1, has_side_effects=True, vmem_limit_bytes=60 << 20
        ),
        cost_estimate=pl.CostEstimate(
            flops=2_500_000_000, bytes_accessed=10_000_000, transcendentals=1_000_000
        ),
        name="kfac_stats",
    )(tokens, hidden_grad, gate, up, gate_weight, up_weight)
    return tuple(
        pl.pallas_call(
            arrange,
            out_shape=(
                jax.ShapeDtypeStruct((256, 128), BF16),
                jax.ShapeDtypeStruct((128, 1024), F32),
                jax.ShapeDtypeStruct((128, 1024), F32),
            ),
            in_specs=[pl.BlockSpec(memory_space=pltpu.VMEM)] * 2,
            out_specs=tuple([pl.BlockSpec(memory_space=pltpu.VMEM)] * 3),
            compiler_params=pltpu.CompilerParams(vmem_limit_bytes=16 << 20),
            name="arrange",
        )(fin, own)
    )


def solution(mesh):
    placed = (
        P("dp", None),
        P("dp", "tensor"),
        P("dp", "tensor"),
        P("dp", "tensor"),
        P("dp", "tensor"),
        P("dp", "tensor"),
    )
    return jax.shard_map(
        shards,
        mesh=mesh,
        in_specs=placed,
        out_specs=(P("dp", "tensor"), P("tensor", None), P("tensor", None)),
        check_vma=False,
    )
```
